32 devices in a mesh: orb: 16 (over z, y, x), trial: 2 (over core).
Axes of the slice: x: 2, y: 2, z: 4, core: 2. Of those that a mesh axis runs over, the one named last changes fastest.
Arguments:
- trials: float32 [4, 64, 4096], P('trial', 'orb'), may hold values from -120 to 120
- orbitals: bfloat16 [32, 64, 4096], P('orb'), may hold values from -6 to 6
- potential: float32 [64, 4096], P('orb'), may hold values from 0.5 to 2
- coulomb: float32 [3, 64, 64], replicated, may hold values from -0.75 to 0.75
- energies: float32 [32], replicated, may hold values from -1.5 to -0.3
- frequencies: float32 [8], replicated, may hold values from 0.3 to 4
- orbital_ids: int32 [32], P('orb'), may hold values from 0 to 31, each once
- freq_index: int32 [32], P('orb'), may hold values from 0 to 7
Outputs:
- filtered: float32 [4, 64, 4096], P('trial', 'orb')
The draws below stay inside these ranges and needn't reach their ends.
All inputs are finite; a program needn't handle non-finite values.
Results may differ from the reference program's by a relative error of at most 0.0003.
Values sent between devices are 32-bit elements; how exact they have to be, the bound alone decides.
No kernel may reach another device: no remote copies, remote signals or barrier semaphores. Data moves between devices by JAX's collectives and lax.ppermute only.
A program may use at most 64 MiB of HBM per device.

```python
import math
import jax
import jax.numpy as jnp
from jax import lax

G = 64
NFREQ = 8
ITERS = 3
ORBS = 32
NTRIAL = 4


def draw_trials(key, part):
    draw_keys = jax.random.split(key, 2)
    shape_full = (NTRIAL, G, G * G)
    plane_scale = (10.0 ** (jnp.arange(G, dtype=jnp.float32) / (G - 1)))[None, :, None]
    cell_scale = jnp.exp(jax.random.uniform(draw_keys[1], shape_full, jnp.float32, 0.0, jnp.log(3.0)))
    base_values = jnp.clip(jax.random.normal(draw_keys[0], shape_full, jnp.float32), -4.0, 4.0)
    return base_values * plane_scale * cell_scale


def with_ends(values, key, low, top_value):
    dims = values.shape
    index_at = [jax.random.randint(jax.random.fold_in(key, axis), (), 0, dims[axis]) for axis in range(len(dims))]
    values = values.at[tuple(index_at)].set(low)
    longest = dims.index(max(dims))
    index_at[longest] = (index_at[longest] + 1) % dims[longest]
    return values.at[tuple(index_at)].set(top_value)


def block_levels(rng, shape, pieces, smallest, high):
    def one(axis_at, blocks):
        steps = jax.random.uniform(jax.random.fold_in(jax.random.fold_in(rng, 6), axis_at), (blocks,), jnp.float32, smallest / len(pieces), high / len(pieces))
        return jnp.repeat(jnp.exp(steps), shape[axis_at] // blocks).reshape((-1,) + (1,) * (len(shape) - axis_at - 1))

    level = one(*pieces[0])
    for cut in pieces[1:]:
        level = level * one(*cut)
    return level


def scatter_about(own_key, shape, width, most, cuts=(), kind=jnp.bfloat16):
    array = width * jax.random.normal(own_key, shape, jnp.float32)
    if cuts:
        array = array * block_levels(own_key, shape, cuts, -0.22, 0.18)
    return jnp.clip(array, -most, most).astype(kind)


def setup_inputs(seed: int = 0) -> dict:
    seeds = jax.random.split(jax.random.key(seed), 9)
    return {
        "trials": draw_trials(jax.random.fold_in(seeds[8], 71), 0),
        "orbitals": scatter_about(seeds[1], (ORBS, G, G * G), 1.0, 6.0, ((0, 16),)),
        "potential": jnp.clip(0.5 + 1.5 * jax.random.uniform(seeds[2], (G, G * G), jnp.float32) ** block_levels(seeds[2], (G, G * G), ((0, 16),), -0.2, 0.2), 0.5, 2.0),
        "coulomb": scatter_about(seeds[3], (3, G, G), G ** -0.5, 0.75, (), jnp.float32),
        "energies": jnp.clip(jax.random.uniform(seeds[4], (ORBS,), jnp.float32, -1.5, -0.3), -1.5, -0.3),
        "frequencies": jnp.clip(jnp.exp(jax.random.uniform(seeds[5], (NFREQ,), jnp.float32, math.log(0.3), math.log(4.0))), 0.3, 4.0),
        "orbital_ids": jax.random.permutation(seeds[6], ORBS).astype(jnp.int32),
        "freq_index": with_ends(jax.random.randint(seeds[7], (ORBS,), 0, NFREQ), jax.random.fold_in(seeds[7], 1), 0, NFREQ - 1).astype(jnp.int32),
    }


def orbital_shifts(orbital_ids, freq_index, energies, frequencies):
    energy_slots = lax.broadcasted_iota(jnp.int32, (1, energies.shape[0]), 1)
    picked_energy = lax.optimization_barrier(jnp.sum(jnp.where(orbital_ids[:, None] == energy_slots, energies[None, :], 0.0), axis=1))
    freq_slots = lax.broadcasted_iota(jnp.int32, (1, frequencies.shape[0]), 1)
    picked_freq = lax.optimization_barrier(jnp.sum(jnp.where(freq_index[:, None] == freq_slots, frequencies[None, :], 0.0), axis=1))
    return picked_freq - picked_energy

def neighbour_sum(grid_field):
    grid_width = grid_field.shape[-2]
    z_index = lax.broadcasted_iota(jnp.int32, (1, grid_field.shape[-1]), 1) % grid_width
    zero_cells = jnp.zeros_like(grid_field[..., :1])
    upper_z = jnp.where(z_index == grid_width - 1, 0.0, jnp.concatenate([grid_field[..., 1:], zero_cells], axis=-1))
    lower_z = jnp.where(z_index == 0, 0.0, jnp.concatenate([zero_cells, grid_field[..., :-1]], axis=-1))
    zero_line = jnp.zeros_like(grid_field[..., :grid_width])
    upper_y = jnp.concatenate([grid_field[..., grid_width:], zero_line], axis=-1)
    lower_y = jnp.concatenate([zero_line, grid_field[..., :-grid_width]], axis=-1)
    zero_plane = jnp.zeros_like(grid_field[..., :1, :])
    upper_x = jnp.concatenate([grid_field[..., 1:, :], zero_plane], axis=-2)
    lower_x = jnp.concatenate([zero_plane, grid_field[..., :-1, :]], axis=-2)
    return upper_z + lower_z + upper_y + lower_y + upper_x + lower_x

def apply_shifted(grid_field, potential, level_shift):
    return (3.0 + potential + level_shift) * grid_field - 0.5 * neighbour_sum(grid_field)

def cell_inner(left_field, right_field):
    return lax.optimization_barrier(jnp.sum(left_field * right_field, axis=(1, 2)))[:, None, None]

def sternheimer(source, potential, level_shift):
    iterate = jnp.zeros_like(source)
    residual = source
    direction = source
    norm_now = cell_inner(residual, residual)
    for sweep_index in range(ITERS):
        mapped = apply_shifted(direction, potential, level_shift)
        step_size = norm_now / cell_inner(direction, mapped)
        iterate = iterate + step_size * direction
        residual = residual - step_size * mapped
        norm_next = cell_inner(residual, residual)
        direction = residual + norm_next / norm_now * direction
        norm_now = norm_next
    return iterate

def orbital_response(whole, orbitals, potential, shifts):

    def one_orbital(accumulated, scanned):
        orbital, level_shift = scanned
        density = orbital.astype(jnp.float32)[None]
        solved = sternheimer(density * whole, potential, level_shift)
        return (accumulated - density * solved, None)
    result, unused = lax.scan(one_orbital, jnp.zeros_like(whole), (orbitals, shifts))
    return result

def coulomb_full(grid_field, factors):
    trial_count = grid_field.shape[0]
    grid_width = grid_field.shape[1]
    cube_view = grid_field.reshape(trial_count, grid_width, grid_width, grid_width)
    cube_view = jnp.einsum('cz,txyz->txyc', factors[2], cube_view, precision=lax.Precision.HIGHEST)
    cube_view = jnp.einsum('by,txyc->txbc', factors[1], cube_view, precision=lax.Precision.HIGHEST)
    cube_view = jnp.einsum('ax,txbc->tabc', factors[0], cube_view, precision=lax.Precision.HIGHEST)
    return cube_view.reshape(trial_count, grid_width, grid_width * grid_width)

def reference(trials, orbitals, potential, coulomb, energies, frequencies, orbital_ids, freq_index):
    shifts = orbital_shifts(orbital_ids, freq_index, energies, frequencies)
    mapped = coulomb_full(orbital_response(trials, orbitals, potential, shifts), coulomb)
    squares = cell_inner(trials, trials)
    center = cell_inner(trials, mapped) / squares
    spread = jnp.sqrt(cell_inner(mapped, mapped) / squares)
    first = (mapped - center * trials) / spread
    second_mapped = coulomb_full(orbital_response(first, orbitals, potential, shifts), coulomb)
    second = 2.0 * (second_mapped - center * first) / spread - trials
    columns = second.reshape(second.shape[0], -1)
    gram_matrix = jnp.dot(columns, columns.T, precision=lax.Precision.HIGHEST) / float(G ** 3)
    lower = jnp.linalg.cholesky(gram_matrix)
    identity = jnp.eye(gram_matrix.shape[0], dtype=gram_matrix.dtype)
    inverse = lax.linalg.triangular_solve(lower, identity, left_side=True, lower=True)
    return jnp.dot(inverse, columns, precision=lax.Precision.HIGHEST).reshape(second.shape)
```

```python
import functools
import jax
import jax.numpy as jnp
from jax import lax
from jax.experimental import pallas as pl
from jax.experimental.pallas import tpu as pltpu
from jax.sharding import PartitionSpec as P

LOW = 2
HIGH = 3
CENTER = 4.25
CHUNK = 16
HIGHEST = lax.Precision.HIGHEST


def orbital_shifts(orbital_ids, freq_index, energies, frequencies):
    energy_slots = lax.broadcasted_iota(jnp.int32, (1, energies.shape[0]), 1)
    picked_energy = jnp.sum(
        jnp.where(orbital_ids[:, None] == energy_slots, energies[None, :], 0.0), axis=1
    )
    freq_slots = lax.broadcasted_iota(jnp.int32, (1, frequencies.shape[0]), 1)
    picked_freq = jnp.sum(
        jnp.where(freq_index[:, None] == freq_slots, frequencies[None, :], 0.0), axis=1
    )
    return picked_freq - picked_energy


def spread_kernel(orbs, rows, src_ref, dst_ref):
    lane = lax.broadcasted_iota(jnp.int32, (orbs, 128), 1)
    first_half = lane < 64

    def body(r8, carry):
        for i in range(8):
            r = r8 * 8 + i
            pair = src_ref[pl.ds(r, orbs, stride=rows), :]
            turned = pltpu.roll(pair, 64, 1)
            dst_ref[2 * r] = jnp.where(first_half, pair, turned)
            dst_ref[2 * r + 1] = jnp.where(first_half, turned, pair)
        return carry

    lax.fori_loop(0, rows // 8, body, 0)


def krylov_kernel(
    slab, lines, grid_width, group,
    flag_ref, o_hbm, v_ref, d_ref, sh_ref,
    u1_hbm, u2_hbm, pay_ref,
    o_s, b_s, u1_s, u2_s, in_sem, out_sem,
):
    window = slab + LOW + HIGH
    lane = lax.broadcasted_iota(jnp.int32, (8, 128), 1) % grid_width
    at_low = lane == 0
    at_high = lane == grid_width - 1
    zero = jnp.zeros((8, 128), jnp.float32)
    pieces = 3
    cuts = [window * k // pieces for k in range(pieces + 1)]
    copies = [
        pltpu.make_async_copy(
            o_hbm.at[pl.ds(cuts[k], cuts[k + 1] - cuts[k])],
            o_s.at[pl.ds(cuts[k], cuts[k + 1] - cuts[k])],
            in_sem.at[k],
        )
        for k in range(pieces)
    ]
    for copy in copies:
        copy.start()

    def clear(w, carry):
        for ref in (b_s, u1_s, u2_s):
            ref[w, 0] = zero
            ref[w, grid_width + 1] = zero
        return carry

    lax.fori_loop(0, window, clear, 0)

    def row_of(ref, w, y0, i):
        per = y0 // lines
        return ref[per + i // lines, pl.ds(w * lines + i % lines, 1), :]

    def products(w, carry):
        def chunk(c, carry):
            y0 = c * CHUNK
            for i in range(CHUNK):
                b_s[w, y0 + i + 1] = o_s[w, y0 + i] * row_of(v_ref, w, y0, i)
            return carry

        return lax.fori_loop(0, grid_width // CHUNK, chunk, carry)

    for k in range(pieces):
        copies[k].wait()
        lax.fori_loop(cuts[k], cuts[k + 1], products, 0)

    def tree(terms):
        while len(terms) > 1:
            terms = [a + b for a, b in zip(terms[::2], terms[1::2])] + (
                [terms[-1]] if len(terms) % 2 else []
            )
        return terms[0]

    def apply(src, dst, w, carry, pairs):
        def chunk(c, carry):
            y0 = c * CHUNK
            rows = [src[w, y0 + i] for i in range(CHUNK + 2)]
            terms = [[] for _ in carry]
            for i in range(CHUNK):
                mid = rows[i + 1]
                around = (rows[i] + rows[i + 2]) + (
                    src[w - 1, y0 + i + 1] + src[w + 1, y0 + i + 1]
                )
                around = around + (
                    jnp.where(at_low, 0.0, pltpu.roll(mid, 1, 1))
                    + jnp.where(at_high, 0.0, pltpu.roll(mid, 127, 1))
                )
                new = row_of(d_ref, w, y0, i) * mid - around
                dst[w, y0 + i + 1] = new
                both = (mid, new)
                for list_at, (a, b) in zip(terms, pairs):
                    list_at.append(both[a] * both[b])
            return tuple(old + tree(t) for old, t in zip(carry, terms))

        return lax.fori_loop(0, grid_width // CHUNK, chunk, carry)

    def wipe(dst, w):
        def chunk(y, carry):
            dst[w, y + 1] = zero
            return carry

        lax.fori_loop(0, grid_width, chunk, 0)

    def halo(src, dst, w, outside):
        @pl.when(outside)
        def _():
            wipe(dst, w)

        @pl.when(jnp.logical_not(outside))
        def _():
            apply(src, dst, w, (), ())

    first = flag_ref[0]
    own = (LOW, LOW + slab)
    halo(b_s, u1_s, LOW - 1, first < 1)
    m0, m1, m2 = lax.fori_loop(
        *own, lambda w, c: apply(b_s, u1_s, w, c, ((0, 0), (0, 1), (1, 1))), (zero,) * 3
    )
    copy_u1 = pltpu.make_async_copy(
        u1_s.at[pl.ds(LOW, slab), pl.ds(1, grid_width)], u1_hbm, out_sem.at[0]
    )
    copy_u1.start()
    halo(b_s, u1_s, LOW + slab, first + slab >= grid_width)
    halo(b_s, u1_s, LOW + slab + 1, first + slab + 1 >= grid_width)
    m3, m4 = lax.fori_loop(
        *own, lambda w, c: apply(u1_s, u2_s, w, c, ((0, 1), (1, 1))), (zero,) * 2
    )
    copy_u2 = pltpu.make_async_copy(
        u2_s.at[pl.ds(LOW, slab), pl.ds(1, grid_width)], u2_hbm, out_sem.at[1]
    )
    copy_u2.start()
    halo(u1_s, u2_s, LOW + slab, first + slab >= grid_width)

    def last(w, carry):
        def chunk(c, carry):
            y0 = c * CHUNK
            rows = [u2_s[w, y0 + i + 1] for i in range(CHUNK + 1)]
            terms = []
            for i in range(CHUNK):
                mid = rows[i]
                above = (rows[i + 1] + u2_s[w + 1, y0 + i + 1]) + jnp.where(
                    at_high, 0.0, pltpu.roll(mid, 127, 1)
                )
                terms.append(mid * (row_of(d_ref, w, y0, i) * mid - 2.0 * above))
            return carry + tree(terms)

        return lax.fori_loop(0, grid_width // CHUNK, chunk, carry)

    m5 = lax.fori_loop(*own, last, zero)
    for k, moment in enumerate((m0, m1, m2, m3, m4, m5)):
        for peer in range(group):
            for row in range(8):
                pay_ref[peer, 8 * k + (row ^ peer) : 8 * k + (row ^ peer) + 1, :] = moment[
                    row : row + 1
                ]
    for peer in range(group):
        pay_ref[peer, 48:56, :] = sh_ref[...]
    copy_u1.wait()
    copy_u2.wait()


def combine_kernel(
    slab, lines, grid_width, group,
    *refs,
):
    pays = refs[:group]
    (v_ref, o_ref, u1_ref, u2_ref, ones_ref, cy_ref, cz_ref, out_ref, coef_s, field_s) = refs[group:]
    step = pl.program_id(0)
    chunks = out_ref.shape[0]

    @pl.when(step == 0)
    def _():
        total = pays[0][0:48]
        for pay in pays[1:]:
            total = total + pay[0:48]
        total = jnp.dot(total, ones_ref[...], precision=HIGHEST, preferred_element_type=jnp.float32)
        halves = 8 // group
        shift = jnp.concatenate(
            [pays[k][48 + half : 49 + half] for half in range(halves) for k in range(group)], axis=0
        )
        m = [total[8 * k : 8 * k + 8] for k in range(6)]
        inv = 1.0 / m[0]
        mu = [None] + [m[k] * inv * (8.0**-k) for k in range(1, 6)]
        sigma = 0.25 * (shift + CENTER)
        k00 = mu[1] + sigma
        k01 = mu[2] + sigma * mu[1]
        k11 = mu[3] + sigma * mu[2]
        k02 = k11
        k12 = mu[4] + sigma * mu[3]
        k22 = mu[5] + sigma * mu[4]
        r0 = 1.0 / k00
        l10 = k01 * r0
        l20 = k02 * r0
        d1 = k11 - l10 * k01
        t = k12 - l20 * k01
        l21 = t / d1
        d2 = k22 - l20 * k02 - l21 * t
        z1 = mu[1] - l10
        z2 = mu[2] - l20 - l21 * z1
        y2 = z2 / d2
        y1 = z1 / d1 - l21 * y2
        y0 = r0 - l10 * y1 - l20 * y2
        coef_s[0] = -0.25 * y0
        coef_s[1] = (-0.25 / 8.0) * y1
        coef_s[2] = (-0.25 / 64.0) * y2

    c0, c1, c2 = coef_s[0], coef_s[1], coef_s[2]
    w = step + LOW
    for y in range(grid_width):
        o = o_ref[0, y]
        b = o * v_ref[y // lines, pl.ds(w * lines + y % lines, 1), :]
        field_s[8 * y : 8 * y + 8, :] = o * (c0 * b + (c1 * u1_ref[0, y] + c2 * u2_ref[0, y]))
    planes = jnp.dot(cy_ref[...], field_s[...], precision=HIGHEST, preferred_element_type=jnp.float32)
    planes = jnp.dot(planes, cz_ref[...], precision=HIGHEST, preferred_element_type=jnp.float32)
    for k in range(chunks):
        out_ref[k, pl.ds(step * lines, lines), :] = planes[k * lines : (k + 1) * lines]


def whole_vmem():
    return pl.BlockSpec(memory_space=pltpu.VMEM)


def shards(n, cores, trials, orbitals, potential, coulomb, energies, frequencies, orbital_ids, freq_index):
    count, planes, cells = trials.shape
    held = orbitals.shape[0]
    width = coulomb.shape[1]
    lines = width // n
    group = 8 // held
    slab = width // group
    window = slab + LOW + HIGH
    send_planes = -(-window * lines // 8) * 8 // lines
    f32 = jnp.float32
    me = lax.axis_index("orb")
    core = lax.axis_index("trial")
    place = me % group
    rows = cells // 128
    each = held // cores

    def swap(x):
        return lax.ppermute(x, "trial", [(k, (k + 1) % cores) for k in range(cores)])

    def peer(x, k):
        return lax.ppermute(x, "orb", [(i, i ^ k) for i in range(n)])

    def exchange(x):
        return lax.all_to_all(x, "orb", split_axis=0, concat_axis=0, tiled=True)

    mine = lax.dynamic_slice_in_dim(orbitals, core * each, each, 0).astype(f32)
    mine = mine.reshape(each, width * rows, 128)
    mine = jnp.pad(mine, ((0, 0), (LOW * rows, HIGH * rows), (0, 0)))
    parts = []
    for k in range(group):
        part = lax.dynamic_slice_in_dim(mine, (place ^ k) * slab * rows, window * rows, 1)
        parts.append(peer(part, k) if k else part)
    own_half = jnp.stack(parts, axis=1).reshape(each * group, window * rows, 128)
    other_half = swap(own_half)
    both = jnp.concatenate([own_half, other_half], axis=0)
    orbs = both.shape[0]
    spread_orbitals = pl.pallas_call(
        functools.partial(spread_kernel, orbs, window * rows),
        out_shape=jax.ShapeDtypeStruct((window * width, orbs, 128), f32),
        in_specs=[whole_vmem()],
        out_specs=whole_vmem(),
        compiler_params=pltpu.CompilerParams(vmem_limit_bytes=40 * 2**20),
        name="spread_orbitals",
    )(both.reshape(orbs * window * rows, 128)).reshape(window, width, orbs, 128)

    shifts = orbital_shifts(orbital_ids, freq_index, energies, frequencies)
    shifts = jnp.where(core == 0, shifts, jnp.roll(shifts, -each))
    shift_rows = jnp.broadcast_to(jnp.pad(shifts, (0, 8 - held))[:, None], (8, 128))

    def lanes(x):
        x = x.reshape(count, planes, width, width)
        return x.transpose(1, 2, 0, 3).reshape(planes, n, lines, 128)

    pot = jnp.broadcast_to(potential[None], (count, planes, cells))
    send = jnp.stack([lanes(trials), lanes(2.0 * (3.0 - CENTER + pot))], 0)
    send = send.transpose(2, 0, 1, 3, 4).reshape(n, 2 * planes * lines, 128)
    got = exchange(send).reshape(n, 2, planes * lines, 128)
    trial_rows = got[:, 0].reshape(width * lines, 128)
    diag_rows = got[:, 1].reshape(width * lines, 128)

    def windows(x):
        x = jnp.pad(x, ((LOW * lines, (send_planes - LOW - slab) * lines), (0, 0)))
        return jnp.stack(
            [x[j * slab * lines : (j * slab + send_planes) * lines] for j in range(group)], 0
        )

    def to_all(x):
        return jnp.tile(x, (n // group, 1, 1))

    size = send_planes * lines
    got = exchange(to_all(jnp.concatenate([windows(trial_rows), windows(diag_rows)], axis=1)))
    trial_window = got[:, :size]
    diag_window = got[:, size:]

    flags = (place * slab).astype(jnp.int32).reshape(1)
    lane_trial = jnp.arange(128) // width
    ones = (lane_trial[:, None] == lane_trial[None, :]).astype(f32)
    cy = jnp.repeat(coulomb[1], orbs, axis=1)
    cz = jnp.kron(jnp.eye(count, dtype=f32), coulomb[2].T)
    cx = jnp.kron(coulomb[0], jnp.eye(lines, dtype=f32))

    def response(v):
        u_shape = jax.ShapeDtypeStruct((slab, width, orbs, 128), f32)
        any_spec = pl.BlockSpec(memory_space=pl.ANY)
        scratch = pltpu.VMEM((window, width + 2, orbs, 128), f32)
        u1, u2, pay = pl.pallas_call(
            functools.partial(krylov_kernel, slab, lines, width, group),
            out_shape=(u_shape, u_shape, jax.ShapeDtypeStruct((group, 56, 128), f32)),
            in_specs=[
                pl.BlockSpec(memory_space=pltpu.SMEM), any_spec, whole_vmem(), whole_vmem(), whole_vmem(),
            ],
            out_specs=(any_spec, any_spec, whole_vmem()),
            scratch_shapes=[
                pltpu.VMEM((window, width, orbs, 128), f32), scratch, scratch, scratch,
                pltpu.SemaphoreType.DMA((3,)), pltpu.SemaphoreType.DMA((2,)),
            ],
            compiler_params=pltpu.CompilerParams(vmem_limit_bytes=48 * 2**20),
            name="krylov",
        )(flags, spread_orbitals, v, diag_window, shift_rows)
        pays = [pay[0]] + [peer(pay[k], k) for k in range(1, group)]
        plane = (1, width, orbs, 128)
        part = pl.pallas_call(
            functools.partial(combine_kernel, slab, lines, width, group),
            grid=(slab,),
            out_shape=jax.ShapeDtypeStruct((n, slab * lines, 128), f32),
            in_specs=[whole_vmem()] * (group + 1)
            + [
                pl.BlockSpec(plane, lambda i: (i + LOW, 0, 0, 0)),
                pl.BlockSpec(plane, lambda i: (i, 0, 0, 0)),
                pl.BlockSpec(plane, lambda i: (i, 0, 0, 0)),
            ]
            + [whole_vmem()] * 3,
            out_specs=pl.BlockSpec((n, slab * lines, 128), lambda i: (0, 0, 0)),
            scratch_shapes=[pltpu.VMEM((3, 8, 128), f32), pltpu.VMEM((8 * width, 128), f32)],
            compiler_params=pltpu.CompilerParams(vmem_limit_bytes=40 * 2**20),
            name="combine",
        )(*pays, v, spread_orbitals, u1, u2, ones, cy, cz)
        got = exchange(part).reshape(n // group, width * lines, 128)
        return jnp.dot(cx, jnp.sum(got, axis=0), precision=HIGHEST)

    def fold(x):
        return jnp.dot(x, ones, precision=HIGHEST)

    mapped = response(trial_window)
    sums = jnp.stack(
        [jnp.sum(a * b, axis=0) for a, b in ((trial_rows, trial_rows), (trial_rows, mapped), (mapped, mapped))], 0
    )
    sums = jnp.broadcast_to(jnp.pad(sums, ((0, 5), (0, 0)))[None], (group, 8, 128))
    got = exchange(to_all(jnp.concatenate([windows(mapped), sums], axis=1)))
    totals = fold(jnp.sum(got[:, size:], axis=0))
    center = totals[1:2] / totals[0:1]
    spread = jnp.sqrt(totals[2:3] / totals[0:1])
    first_window = (got[:, :size] - center * trial_window) / spread
    first = (mapped - center * trial_rows) / spread
    second = 2.0 * (response(first_window) - center * first) / spread - trial_rows
    other = swap(second)

    def turn(x):
        return jnp.concatenate([x[..., width:], x[..., :width]], axis=-1)

    pairs = (
        (second, second), (second, turn(second)), (second, other), (second, turn(other)), (other, other), (other, turn(other)),
    )
    sums = jnp.pad(jnp.stack([jnp.sum(a * b, axis=0) for a, b in pairs], 0), ((0, 2), (0, 0)))
    sums = jnp.broadcast_to(sums[None], (n, 8, 128))
    per = planes * lines
    got = exchange(jnp.concatenate([second.reshape(n, per, 128), sums], axis=1))
    block = got[:, :per]
    block_other = swap(block)
    gram = fold(jnp.sum(got[:, per:], axis=0)) / float(width * width * width)
    s = [[gram[k, 0], gram[k, width]] for k in range(6)]
    aa = ((s[0][0], s[1][0]), (s[1][0], s[0][1]))
    bb = ((s[4][0], s[5][0]), (s[5][0], s[4][1]))
    ab = ((s[2][0], s[3][0]), (s[3][1], s[2][1]))
    is_low = core == 0
    matrix = [[None] * 4 for _ in range(4)]
    for i in range(2):
        for j in range(2):
            matrix[i][j] = jnp.where(is_low, aa[i][j], bb[i][j])
            matrix[2 + i][2 + j] = jnp.where(is_low, bb[i][j], aa[i][j])
            matrix[i][2 + j] = jnp.where(is_low, ab[i][j], ab[j][i])
            matrix[2 + j][i] = matrix[i][2 + j]
    size4 = 4
    low = [[None] * size4 for _ in range(size4)]
    inverse = [[jnp.float32(0)] * size4 for _ in range(size4)]
    for i in range(size4):
        for j in range(i + 1):
            value = matrix[i][j] - sum((low[i][k] * low[j][k] for k in range(j)), jnp.float32(0))
            low[i][j] = jnp.sqrt(value) if i == j else value / low[j][j]
    for j in range(size4):
        inverse[j][j] = 1.0 / low[j][j]
        for i in range(j + 1, size4):
            inverse[i][j] = -sum((low[i][k] * inverse[k][j] for k in range(j, i)), jnp.float32(0)) / low[i][i]

    def pick(i, j):
        top = inverse[i][j]
        here, there = (j, (j + 2) % 4)
        return jnp.where(is_low, top if i < 2 else 0.0, inverse[i + 2][there])

    def spread_lanes(a, b):
        return jnp.where(lane_trial == 0, a, b)[None, None, :]

    result = (
        spread_lanes(pick(0, 0), pick(1, 1)) * block
        + spread_lanes(pick(0, 1), pick(1, 0)) * turn(block)
        + spread_lanes(pick(0, 2), pick(1, 3)) * block_other
        + spread_lanes(pick(0, 3), pick(1, 2)) * turn(block_other)
    )
    result = result.reshape(n, planes, lines, count, width).transpose(3, 1, 0, 2, 4)
    return result.reshape(count, planes, cells)


def solution(mesh):
    n, cores = mesh.shape["orb"], mesh.shape["trial"]
    in_specs = (
        P("trial", "orb", None), P("orb", None, None), P("orb", None), P(), P(), P(), P("orb"), P("orb"),
    )
    return jax.shard_map(
        functools.partial(shards, n, cores),
        mesh=mesh, in_specs=in_specs, out_specs=P("trial", "orb", None), check_vma=False,
    )
```

```python
import functools
import jax
import jax.numpy as jnp
from jax import lax
from jax.experimental import pallas as pl
from jax.experimental.pallas import tpu as pltpu
from jax.sharding import PartitionSpec as P

LOW = 2
HIGH = 3
CENTER = 4.25
ORBS = 16
SHIFT_LANE = 12
MOMENTS = 6
HIGHEST = lax.Precision.HIGHEST
F32 = jnp.float32
MIB = 2**20


def dot(a, b):
    return jnp.dot(a, b, precision=HIGHEST, preferred_element_type=F32)


def halves(rows, width, value=1.0):
    a = lax.broadcasted_iota(jnp.int32, (128, 128), 0) // width
    b = lax.broadcasted_iota(jnp.int32, (128, 128), 1) // width
    return jnp.where(a == b, 1.0, 0.0)


def tree(terms):
    while len(terms) > 1:
        odd = [terms[-1]] if len(terms) % 2 else []
        terms = [a + b for a, b in zip(terms[::2], terms[1::2])] + odd
    return terms[0]


def orbital_shifts(orbital_ids, freq_index, energies, frequencies):
    energy_slots = lax.broadcasted_iota(jnp.int32, (1, energies.shape[0]), 1)
    picked_energy = jnp.sum(
        jnp.where(orbital_ids[:, None] == energy_slots, energies[None, :], 0.0), axis=1
    )
    freq_slots = lax.broadcasted_iota(jnp.int32, (1, frequencies.shape[0]), 1)
    picked_freq = jnp.sum(
        jnp.where(freq_index[:, None] == freq_slots, frequencies[None, :], 0.0), axis=1
    )
    return picked_freq - picked_energy


def spread_kernel(window, pairs, own_ref, other_ref, dst_ref):
    half = ORBS // 2
    rows = window * pairs
    first_half = lax.broadcasted_iota(jnp.int32, (ORBS, 128), 1) < 64

    def body(w, carry):
        for i in range(pairs):
            at = pl.ds(w * pairs + i, half, stride=rows)
            pair = jnp.concatenate([own_ref[at, :], other_ref[at, :]], axis=0)
            turned = pltpu.roll(pair, 64, 1)
            dst_ref[w, 2 * i] = jnp.where(first_half, pair, turned).astype(jnp.bfloat16)
            dst_ref[w, 2 * i + 1] = jnp.where(first_half, turned, pair).astype(jnp.bfloat16)
        return carry

    lax.fori_loop(0, window, body, 0)


def krylov_kernel(slab, lines, width, group, filtered, *refs):
    flag_ref, o_ref, d_ref, sh_ref, t_ref = refs[:5]
    if filtered:
        m_ref, u1_ref, u2_ref, pay_ref, v_ref, cs_ref, b_s = refs[5:]
    else:
        u1_ref, u2_ref, pay_ref, b_s = refs[5:]
        v_ref = t_ref
    window = slab + LOW + HIGH
    lane = lax.broadcasted_iota(jnp.int32, (ORBS, 128), 1)
    at_low = lane % width == 0
    at_high = lane % width == width - 1
    zero = jnp.zeros((ORBS, 128), F32)
    n = t_ref.shape[0]

    if filtered:
        base = m_ref.shape[1] - 8
        total = m_ref[0, base : base + 8, :]
        for k in range(1, n):
            total = total + m_ref[k, base : base + 8, :]
        total = dot(total, halves(8, width))
        center = total[1:2] / total[0:1]
        inverse = 1.0 / jnp.sqrt(total[2:3] / total[0:1])
        cs_ref[0:1] = center
        cs_ref[1:2] = inverse
        used = v_ref.shape[1]
        for k in range(n):
            v_ref[k] = (m_ref[k, 0:used, :] - center * t_ref[k, 0:used, :]) * inverse

    def v_row(w, y):
        return v_ref[y // lines, pl.ds(w * lines + y % lines, 1), :]

    def d_row(w, y):
        return d_ref[y % lines, y // lines, pl.ds(w, 1), :]

    def products(w, carry):
        for y in range(width):
            b_s[w, y] = o_ref[w, y].astype(F32) * v_row(w, y)
        return carry

    lax.fori_loop(0, window, products, 0)

    def apply(src, src_at, dst, dst_at, w, carry, pairs):
        rows = [zero] + [src[w - src_at, y] for y in range(width)] + [zero]
        terms = [[] for _ in carry]
        for y in range(width):
            mid = rows[y + 1]
            around = (rows[y] + rows[y + 2]) + (src[w - 1 - src_at, y] + src[w + 1 - src_at, y])
            around = around + (
                jnp.where(at_low, 0.0, pltpu.roll(mid, 1, 1))
                + jnp.where(at_high, 0.0, pltpu.roll(mid, 127, 1))
            )
            new = d_row(w, y) * mid - around
            dst[w - dst_at, y] = new
            both = (mid, new)
            for list_at, (a, b) in zip(terms, pairs):
                list_at.append(both[a] * both[b])
        return tuple(old + tree(t) for old, t in zip(carry, terms))

    def halo(src, src_at, dst, dst_at, w, outside):
        @pl.when(outside)
        def _():
            dst[w - dst_at] = jnp.zeros((width, ORBS, 128), F32)

        @pl.when(jnp.logical_not(outside))
        def _():
            apply(src, src_at, dst, dst_at, w, (), ())

    first = flag_ref[0]
    own = (LOW, LOW + slab)
    halo(b_s, 0, u1_ref, 1, LOW - 1, first < 1)
    m0, m1, m2 = lax.fori_loop(
        *own, lambda w, c: apply(b_s, 0, u1_ref, 1, w, c, ((0, 0), (0, 1), (1, 1))), (zero,) * 3
    )
    halo(b_s, 0, u1_ref, 1, LOW + slab, first + slab >= width)
    halo(b_s, 0, u1_ref, 1, LOW + slab + 1, first + slab + 1 >= width)
    m3, m4 = lax.fori_loop(
        *own, lambda w, c: apply(u1_ref, 1, u2_ref, LOW, w, c, ((0, 1), (1, 1))), (zero,) * 2
    )
    halo(u1_ref, 1, u2_ref, LOW, LOW + slab, first + slab >= width)

    def last(w, carry):
        rows = [u2_ref[w - LOW, y] for y in range(width)] + [zero]
        terms = []
        for y in range(width):
            mid = rows[y]
            above = (rows[y + 1] + u2_ref[w + 1 - LOW, y]) + jnp.where(
                at_high, 0.0, pltpu.roll(mid, 127, 1)
            )
            terms.append(mid * (d_row(w, y) * mid - 2.0 * above))
        return carry + tree(terms)

    m5 = lax.fori_loop(*own, last, zero)
    column = lax.broadcasted_iota(jnp.int32, (128, 128), 1)
    half = lax.broadcasted_iota(jnp.int32, (128, 128), 0) // width
    packed = sh_ref[...]
    for k, moment in enumerate((m0, m1, m2, m3, m4, m5)):
        packed = packed + dot(moment, jnp.where(column == 2 * k + half, 1.0, 0.0))
    for peer in range(group):
        pay_ref[peer] = packed


def combine_kernel(slab, lines, width, group, pay_ref, v_ref, o_ref, u1_ref, u2_ref, cy_ref, cz_ref, out_ref, field_s):
    chunks = out_ref.shape[0]
    total = pay_ref[0]
    for k in range(1, group):
        total = total + pay_ref[k]
    row = lax.broadcasted_iota(jnp.int32, (128, 128), 0)
    half = lax.broadcasted_iota(jnp.int32, (128, 128), 1) // width
    m = [dot(total, jnp.where(row == 2 * k + half, 1.0, 0.0)) for k in range(MOMENTS)]
    shift = dot(total, jnp.where(row == SHIFT_LANE, 1.0, 0.0))
    inv = 1.0 / m[0]
    mu = [None] + [m[k] * inv * (8.0**-k) for k in range(1, MOMENTS)]
    sigma = 0.25 * (shift + CENTER)
    k00 = mu[1] + sigma
    k01 = mu[2] + sigma * mu[1]
    k11 = mu[3] + sigma * mu[2]
    k02 = k11
    k12 = mu[4] + sigma * mu[3]
    k22 = mu[5] + sigma * mu[4]
    r0 = 1.0 / k00
    l10 = k01 * r0
    l20 = k02 * r0
    d1 = k11 - l10 * k01
    t = k12 - l20 * k01
    l21 = t / d1
    d2 = k22 - l20 * k02 - l21 * t
    z1 = mu[1] - l10
    z2 = mu[2] - l20 - l21 * z1
    y2 = z2 / d2
    y1 = z1 / d1 - l21 * y2
    y0 = r0 - l10 * y1 - l20 * y2
    c0 = -0.25 * y0
    c1 = (-0.25 / 8.0) * y1
    c2 = (-0.25 / 64.0) * y2

    def plane(x, carry):
        w = x + LOW
        for y in range(width):
            o = o_ref[w, y].astype(F32)
            b = o * v_ref[y // lines, pl.ds(w * lines + y % lines, 1), :]
            share = o * (c0 * b + (c1 * u1_ref[x + LOW - 1, y] + c2 * u2_ref[x, y]))
            field_s[8 * y : 8 * y + 8, :] = share[0:8] + share[8:16]
        planes = dot(dot(cy_ref[...], field_s[...]), cz_ref[...])
        for k in range(chunks):
            out_ref[k, pl.ds(x * lines, lines), :] = planes[k * lines : (k + 1) * lines]
        return carry

    lax.fori_loop(0, slab, plane, 0)


def gathered(got_ref, cx_ref, group):
    n, rows, _ = got_ref.shape
    parts = []
    for j in range(group):
        parts.append(tree([got_ref[q * group + j] for q in range(n // group)]))
    return dot(cx_ref[...], jnp.concatenate(parts, axis=0))


def mapped_kernel(slab, lines, width, group, got_ref, cx_ref, t_ref, mapped_ref, pay_ref):
    n, size, _ = pay_ref.shape
    mapped = gathered(got_ref, cx_ref, group)
    mapped_ref[...] = mapped
    t = t_ref[...]
    sums = [jnp.sum(a * b, axis=0, keepdims=True) for a, b in ((t, t), (t, mapped), (mapped, mapped))]
    window = (slab + LOW + HIGH) * lines
    for k in range(n):
        start = (k % group) * slab * lines - LOW * lines
        low, high = max(start, 0), min(start + window, width * lines)
        pay_ref[k] = jnp.zeros((size, 128), F32)
        pay_ref[k, low - start : high - start, :] = mapped_ref[low:high, :]
        for i, s in enumerate(sums):
            pay_ref[k, size - 8 + i : size - 7 + i, :] = s


def second_kernel(group, got_ref, cx_ref, t_ref, mapped_ref, cs_ref, second_ref):
    again = gathered(got_ref, cx_ref, group)
    center, inverse = cs_ref[0:1], cs_ref[1:2]
    t = t_ref[...]
    first = (mapped_ref[...] - center * t) * inverse
    second_ref[...] = 2.0 * (again - center * first) * inverse - t


def turn(x):
    return pltpu.roll(x, 64, x.ndim - 1)


def gram_kernel(per, second_ref, other_ref, pay_ref):
    n, size, _ = pay_ref.shape
    a, b = second_ref[...], other_ref[...]
    a1, b1 = turn(a), turn(b)
    pairs = ((a, a), (a, a1), (a, b), (a, b1), (b, b), (b, b1))
    sums = [jnp.sum(p * q, axis=0, keepdims=True) for p, q in pairs]
    block = jnp.concatenate(sums + [jnp.zeros((8 - len(sums), 128), F32)], axis=0)
    for k in range(n):
        pay_ref[k, 0:per, :] = second_ref[k * per : (k + 1) * per, :]
        pay_ref[k, size - 8 : size, :] = block


def final_kernel(per, width, flag_ref, got_ref, other_ref, out_ref):
    n, size, _ = got_ref.shape
    total = tree([got_ref[k, size - 8 : size, :] for k in range(n)])
    total = dot(total, halves(8, width)) / float(width**3)
    swapped = turn(total)
    lane = lax.broadcasted_iota(jnp.int32, (1, 128), 1)
    in_first = lane < width
    is_low = jnp.zeros((1, 128), jnp.int32) + flag_ref[1] == 0

    def entry(k, t):
        here, there = total[k : k + 1], swapped[k : k + 1]
        return jnp.where(in_first, here, there) if t == 0 else jnp.where(in_first, there, here)

    aa = ((entry(0, 0), entry(1, 0)), (entry(1, 0), entry(0, 1)))
    bb = ((entry(4, 0), entry(5, 0)), (entry(5, 0), entry(4, 1)))
    ab = ((entry(2, 0), entry(3, 0)), (entry(3, 1), entry(2, 1)))
    m = [[None] * 4 for _ in range(4)]
    for i in range(2):
        for j in range(2):
            m[i][j] = jnp.where(is_low, aa[i][j], bb[i][j])
            m[2 + i][2 + j] = jnp.where(is_low, bb[i][j], aa[i][j])
            m[2 + j][i] = jnp.where(is_low, ab[i][j], ab[j][i])
    low = [[None] * 4 for _ in range(4)]
    inv = [[jnp.zeros((1, 128), F32)] * 4 for _ in range(4)]
    for j in range(4):
        pivot = m[j][j]
        for k in range(j):
            pivot = pivot - low[j][k] * low[j][k]
        inv[j][j] = 1.0 / jnp.sqrt(pivot)
        for i in range(j + 1, 4):
            value = m[i][j]
            for k in range(j):
                value = value - low[i][k] * low[j][k]
            low[i][j] = value * inv[j][j]
    for j in range(4):
        for i in range(j + 1, 4):
            value = low[i][j] * inv[j][j]
            for k in range(j + 1, i):
                value = value + low[i][k] * inv[k][j]
            inv[i][j] = -value * inv[i][i]

    def pick(i, j):
        return jnp.where(is_low, inv[i][j], inv[2 + i][(j + 2) % 4])

    c = [
        jnp.where(in_first, pick(0, a), pick(1, b)) for a, b in ((0, 1), (1, 0), (2, 3), (3, 2))
    ]
    for k in range(n):
        a, b = got_ref[k, 0:per, :], other_ref[k]
        out_ref[k] = (c[0] * a + c[1] * turn(a)) + (c[2] * b + c[3] * turn(b))


def vmem():
    return pl.BlockSpec(memory_space=pltpu.VMEM)


def smem():
    return pl.BlockSpec(memory_space=pltpu.SMEM)


def call(kernel, name, shapes, inputs, scratch=(), limit=16, in_smem=()):
    return pl.pallas_call(
        kernel,
        out_shape=shapes,
        in_specs=[smem() if k in in_smem else vmem() for k in range(len(inputs))],
        out_specs=jax.tree.map(lambda _: vmem(), shapes),
        scratch_shapes=scratch,
        compiler_params=pltpu.CompilerParams(vmem_limit_bytes=limit * MIB),
        name=name,
    )(*inputs)


def shape(*dims):
    return jax.ShapeDtypeStruct(dims, F32)


def up8(x):
    return -(-x // 8) * 8


def shards(n, cores, trials, orbitals, potential, coulomb, energies, frequencies, orbital_ids, freq_index):
    count, planes, cells = trials.shape
    held = orbitals.shape[0]
    width = coulomb.shape[1]
    lines = width // n
    group = ORBS // held
    slab = width // group
    window = slab + LOW + HIGH
    me = lax.axis_index("orb")
    core = lax.axis_index("trial")
    place = me % group
    pairs = cells // 128
    each = held // cores
    groups = [list(range(q * group, (q + 1) * group)) for q in range(n // group)]

    def swap(x):
        return lax.ppermute(x, "trial", [(k, (k + 1) % cores) for k in range(cores)])

    def exchange(x):
        return lax.all_to_all(x, "orb", split_axis=0, concat_axis=0, tiled=True)

    def exchange_group(x):
        return lax.all_to_all(
            x, "orb", split_axis=0, concat_axis=0, tiled=True, axis_index_groups=groups
        )

    mine = lax.dynamic_slice_in_dim(orbitals, core * each, each, 0).astype(F32)
    mine = mine.reshape(each, width * pairs, 128)
    mine = jnp.pad(mine, ((0, 0), (LOW * pairs, HIGH * pairs), (0, 0)))
    sent = jnp.stack(
        [mine[:, j * slab * pairs : (j * slab + window) * pairs] for j in range(group)], axis=0
    )
    own_half = exchange_group(sent.reshape(group, each * window * pairs, 128))
    own_half = own_half.reshape(ORBS // 2 * window * pairs, 128)
    other_half = swap(own_half)
    spread_orbitals = call(
        functools.partial(spread_kernel, window, pairs),
        "spread_orbitals",
        jax.ShapeDtypeStruct((window, width, ORBS, 128), jnp.bfloat16),
        (own_half, other_half),
        limit=16,
    )
    shifts = orbital_shifts(orbital_ids, freq_index, energies, frequencies)
    shifts = jnp.where(core == 0, shifts, jnp.roll(shifts, -each))
    slot_rows = [(k // each) * (ORBS // 2) + place * each + k % each for k in range(held)]
    row = lax.broadcasted_iota(jnp.int32, (ORBS, 128), 0)
    lane = lax.broadcasted_iota(jnp.int32, (ORBS, 128), 1)
    shift_rows = sum(
        jnp.where((row == slot_rows[k]) & (lane == SHIFT_LANE), shifts[k], 0.0) for k in range(held)
    )

    t_rows = trials.reshape(count, planes, width, width).transpose(1, 2, 0, 3)
    t_rows = t_rows.reshape(planes, n, lines, 128).transpose(1, 0, 2, 3).reshape(n, planes * lines, 128)
    diag = 2.0 * (3.0 - CENTER + potential)
    shared = lines % (2 * cores) == 0
    kept = lines // 2 // cores if shared else lines
    if shared:
        d_rows = diag.reshape(planes, n, cores, kept, 128)
        d_rows = lax.dynamic_index_in_dim(d_rows, core, 2, keepdims=False)
    else:
        d_rows = jnp.tile(diag.reshape(planes, n, lines, width), (1, 1, 1, 128 // width))
    d_rows = d_rows.transpose(1, 0, 2, 3).reshape(n, planes * kept, 128)
    got = exchange(jnp.concatenate([t_rows, d_rows], axis=1))
    trial_rows = got[:, : planes * lines].reshape(width * lines, 128)
    diag_rows = got[:, planes * lines :].reshape(width * kept, 128)

    def windows(x, per):
        x = jnp.pad(x, ((LOW * per, HIGH * per), (0, 0)))
        return jnp.stack([x[j * slab * per : (j * slab + window) * per] for j in range(group)], 0)

    used = window * lines
    size = up8(used + window * kept)
    both = jnp.concatenate([windows(trial_rows, lines), windows(diag_rows, kept)], axis=1)
    both = jnp.pad(both, ((0, 0), (0, size - both.shape[1]), (0, 0)))
    trial_window = exchange(jnp.tile(both, (n // group, 1, 1)))
    diag_own = trial_window[:, used : used + window * kept].reshape(n, window, kept, 128)
    diag_own = diag_own.transpose(2, 0, 1, 3)
    if shared:
        diag_other = swap(diag_own)
        low, high = jnp.where(core == 0, diag_own, diag_other), jnp.where(core == 0, diag_other, diag_own)
        both = jnp.concatenate([low, high], axis=0)
        both = jnp.stack(
            [jnp.tile(both[..., h * width : (h + 1) * width], (1, 1, 1, 2)) for h in range(2)], axis=1
        )
        diag_window = both.reshape(lines, n, window, 128)
    else:
        diag_window = diag_own

    flags = jnp.stack([place * slab, core]).astype(jnp.int32)
    cy = jnp.repeat(coulomb[1], 8, axis=1)
    cz = jnp.kron(jnp.eye(count, dtype=F32), coulomb[2].T)
    wide = lax.broadcasted_iota(jnp.int32, (width * lines, width), 0) // lines
    wide = (wide == lax.broadcasted_iota(jnp.int32, (width * lines, width), 1)).astype(F32)
    cx = jnp.dot(jnp.dot(wide, coulomb[0], precision=HIGHEST), wide.T, precision=HIGHEST)
    a = lax.broadcasted_iota(jnp.int32, cx.shape, 0) % lines
    b = lax.broadcasted_iota(jnp.int32, cx.shape, 1) % lines
    cx = jnp.where(a == b, cx, 0.0)

    def response(fields):
        filtered = len(fields) == 2
        shapes = [
            shape(slab + 3, width, ORBS, 128), shape(slab + 1, width, ORBS, 128), shape(group, ORBS, 128),
        ]
        if filtered:
            shapes += [shape(n, used, 128), shape(8, 128)]
        made = call(
            functools.partial(krylov_kernel, slab, lines, width, group, filtered),
            "krylov",
            tuple(shapes),
            (flags, spread_orbitals, diag_window, shift_rows, *fields),
            scratch=[pltpu.VMEM((window, width, ORBS, 128), F32)],
            limit=32,
            in_smem=(0,),
        )
        u1, u2, pay = made[:3]
        v = made[3] if filtered else fields[0]
        part = call(
            functools.partial(combine_kernel, slab, lines, width, group),
            "combine",
            shape(n, slab * lines, 128),
            (exchange_group(pay), v, spread_orbitals, u1, u2, cy, cz),
            scratch=[pltpu.VMEM((8 * width, 128), F32)],
            limit=32,
        )
        return exchange(part), (made[4] if filtered else None)

    got, _ = response((trial_window,))
    mapped, pay = call(
        functools.partial(mapped_kernel, slab, lines, width, group),
        "mapped",
        (shape(width * lines, 128), shape(n, up8(used) + 8, 128)),
        (got, cx, trial_rows),
    )
    got, scales = response((trial_window, exchange(pay)))
    second = call(
        functools.partial(second_kernel, group),
        "second",
        shape(width * lines, 128),
        (got, cx, trial_rows, mapped, scales),
    )
    per = planes * lines
    pay = call(functools.partial(gram_kernel, per), "gram", shape(n, up8(per) + 8, 128), (second, swap(second)))
    got = exchange(pay)
    result = call(
        functools.partial(final_kernel, per, width),
        "final",
        shape(n, per, 128),
        (flags, got, swap(got[:, :per])),
        in_smem=(0,),
    )
    result = result.reshape(n, planes, lines, count, width).transpose(3, 1, 0, 2, 4)
    return result.reshape(count, planes, cells)


def solution(mesh):
    n, cores = mesh.shape["orb"], mesh.shape["trial"]
    in_specs = (
        P("trial", "orb", None), P("orb", None, None), P("orb", None), P(), P(), P(), P("orb"), P("orb"),
    )
    return jax.shard_map(
        functools.partial(shards, n, cores),
        mesh=mesh, in_specs=in_specs, out_specs=P("trial", "orb", None), check_vma=False,
    )
```

```python
import functools
import jax
import jax.numpy as jnp
from jax import lax
from jax.experimental import pallas as pl
from jax.experimental.pallas import tpu as pltpu
from jax.sharding import PartitionSpec as P

LOW = 2
HIGH = 3
CENTER = 4.25
ORBS = 16
SHIFT_LANE = 12
MOMENTS = 6
HIGHEST = lax.Precision.HIGHEST
F32 = jnp.float32
MIB = 2**20


def dot(a, b):
    return jnp.dot(a, b, precision=HIGHEST, preferred_element_type=F32)


def halves(rows, width, value=1.0):
    a = lax.broadcasted_iota(jnp.int32, (128, 128), 0) // width
    b = lax.broadcasted_iota(jnp.int32, (128, 128), 1) // width
    return jnp.where(a == b, 1.0, 0.0)


def tree(terms):
    while len(terms) > 1:
        odd = [terms[-1]] if len(terms) % 2 else []
        terms = [a + b for a, b in zip(terms[::2], terms[1::2])] + odd
    return terms[0]


def orbital_shifts(orbital_ids, freq_index, energies, frequencies):
    energy_slots = lax.broadcasted_iota(jnp.int32, (1, energies.shape[0]), 1)
    picked_energy = jnp.sum(
        jnp.where(orbital_ids[:, None] == energy_slots, energies[None, :], 0.0), axis=1
    )
    freq_slots = lax.broadcasted_iota(jnp.int32, (1, frequencies.shape[0]), 1)
    picked_freq = jnp.sum(
        jnp.where(freq_index[:, None] == freq_slots, frequencies[None, :], 0.0), axis=1
    )
    return picked_freq - picked_energy


def spread_kernel(window, pairs, own_ref, other_ref, dst_ref):
    half = ORBS // 2
    rows = window * pairs
    first_half = lax.broadcasted_iota(jnp.int32, (ORBS, 128), 1) < 64

    def body(w, carry):
        for i in range(pairs):
            at = pl.ds(w * pairs + i, half, stride=rows)
            pair = jnp.concatenate([own_ref[at, :], other_ref[at, :]], axis=0)
            turned = pltpu.roll(pair, 64, 1)
            dst_ref[w, 2 * i] = jnp.where(first_half, pair, turned).astype(jnp.bfloat16)
            dst_ref[w, 2 * i + 1] = jnp.where(first_half, turned, pair).astype(jnp.bfloat16)
        return carry

    lax.fori_loop(0, window, body, 0)


def pack_kernel(slab, window, width, pairs, src_ref, dst_ref):
    each = src_ref.shape[0]
    size = window * pairs
    for j in range(dst_ref.shape[0]):
        start = (j * slab - LOW) * pairs
        low, high = max(start, 0), min(start + size, width * pairs)
        for e in range(each):
            if low > start:
                dst_ref[j, e * size : e * size + low - start, :] = jnp.zeros((low - start, 128), F32)
            if high < start + size:
                dst_ref[j, e * size + high - start : (e + 1) * size, :] = jnp.zeros(
                    (start + size - high, 128), F32
                )
            dst_ref[j, e * size + low - start : e * size + high - start, :] = src_ref[e, low:high, :]


def equal(rows, columns, left, right):
    a = lax.broadcasted_iota(jnp.int32, (rows, columns), 0)
    b = lax.broadcasted_iota(jnp.int32, (rows, columns), 1)
    return left(a) == right(b)


def factors_kernel(lines, width, c_ref, cx_ref, cy_ref, cz_ref):
    size = width * lines
    pick = jnp.where(equal(size, width, lambda a: a // lines, lambda b: b), 1.0, 0.0)
    turned = jnp.where(equal(width, size, lambda a: a, lambda b: b // lines), 1.0, 0.0)
    same = equal(size, size, lambda a: a % lines, lambda b: b % lines)
    cx_ref[...] = jnp.where(same, dot(dot(pick, c_ref[0]), turned), 0.0)
    eight = jnp.where(equal(width, 8 * width, lambda a: a, lambda b: b // 8), 1.0, 0.0)
    cy_ref[...] = dot(c_ref[1], eight)
    pick = jnp.where(equal(128, width, lambda a: a % width, lambda b: b), 1.0, 0.0)
    turned = jnp.where(equal(width, 128, lambda a: a, lambda b: b % width), 1.0, 0.0)
    same = equal(128, 128, lambda a: a // width, lambda b: b // width)
    cz_ref[...] = jnp.where(same, dot(dot(pick, c_ref[2].T), turned), 0.0)


def slab_kernel(rounds, flag_ref, *refs):
    dst_ref = refs[rounds]
    rows = refs[0].shape[1]
    for r in range(rounds):
        k = lax.rem(flag_ref[2] - r + rounds, rounds)
        dst_ref[:, pl.ds(pl.multiple_of(k * rows, 8), rows), :] = refs[r][...]


def fields_kernel(slab, lines, pairs, slab_ref, low_ref, high_ref, v_ref, d_ref):
    first_half = lax.broadcasted_iota(jnp.int32, (8, 128), 1) < 64

    def both(a, b):
        return jnp.where(first_half, a, turn(b)), jnp.where(first_half, turn(a), b)

    for w in range(slab + LOW + HIGH):
        if w < LOW:
            ref, at = low_ref, w
        elif w < LOW + slab:
            ref, at = slab_ref, w - LOW
        else:
            ref, at = high_ref, w - LOW - slab
        for rb in range(pairs // 8):
            rows = slice(at * pairs + 8 * rb, at * pairs + 8 * rb + 8)
            v = both(ref[0, rows, :], ref[1, rows, :])
            diag = 2.0 * (3.0 - CENTER + ref[2, rows, :])
            d = both(diag, diag)
            for i in range(8):
                for h in range(2):
                    y = 2 * (8 * rb + i) + h
                    row = w * lines + y % lines
                    v_ref[y // lines, row : row + 1, :] = v[h][i : i + 1]
                    d_ref[y // lines, row : row + 1, :] = d[h][i : i + 1]


def krylov_kernel(slab, lines, width, group, filtered, *refs):
    flag_ref, o_ref, d_ref, sh_ref, t_ref = refs[:5]
    if filtered:
        m_ref, u1_ref, u2_ref, pay_ref, v_ref, cs_ref, b_s = refs[5:]
    else:
        u1_ref, u2_ref, pay_ref, b_s = refs[5:]
        v_ref = t_ref
    window = slab + LOW + HIGH
    lane = lax.broadcasted_iota(jnp.int32, (ORBS, 128), 1)
    at_low = lane % width == 0
    at_high = lane % width == width - 1
    zero = jnp.zeros((ORBS, 128), F32)
    n = t_ref.shape[0]

    if filtered:
        base = m_ref.shape[1] - 8
        total = m_ref[0, base : base + 8, :]
        for k in range(1, n):
            total = total + m_ref[k, base : base + 8, :]
        total = dot(total, halves(8, width))
        center = total[1:2] / total[0:1]
        inverse = 1.0 / jnp.sqrt(total[2:3] / total[0:1])
        cs_ref[0:1] = center
        cs_ref[1:2] = inverse
        used = v_ref.shape[1]
        for k in range(n):
            v_ref[k] = (m_ref[k, 0:used, :] - center * t_ref[k, 0:used, :]) * inverse

    def v_row(w, y):
        return v_ref[y // lines, pl.ds(w * lines + y % lines, 1), :]

    def d_row(w, y):
        return d_ref[y // lines, pl.ds(w * lines + y % lines, 1), :]

    def products(w, carry):
        for y in range(width):
            b_s[w, y] = o_ref[w, y].astype(F32) * v_row(w, y)
        return carry

    lax.fori_loop(0, window, products, 0)

    def apply(src, src_at, dst, dst_at, w, carry, pairs):
        rows = [zero] + [src[w - src_at, y] for y in range(width)] + [zero]
        terms = [[] for _ in carry]
        for y in range(width):
            mid = rows[y + 1]
            around = (rows[y] + rows[y + 2]) + (src[w - 1 - src_at, y] + src[w + 1 - src_at, y])
            around = around + (
                jnp.where(at_low, 0.0, pltpu.roll(mid, 1, 1))
                + jnp.where(at_high, 0.0, pltpu.roll(mid, 127, 1))
            )
            new = d_row(w, y) * mid - around
            dst[w - dst_at, y] = new
            both = (mid, new)
            for list_at, (a, b) in zip(terms, pairs):
                list_at.append(both[a] * both[b])
        return tuple(old + tree(t) for old, t in zip(carry, terms))

    def halo(src, src_at, dst, dst_at, w, outside):
        @pl.when(outside)
        def _():
            dst[w - dst_at] = jnp.zeros((width, ORBS, 128), F32)

        @pl.when(jnp.logical_not(outside))
        def _():
            apply(src, src_at, dst, dst_at, w, (), ())

    first = flag_ref[0]
    own = (LOW, LOW + slab)
    halo(b_s, 0, u1_ref, 1, LOW - 1, first < 1)
    m0, m1, m2 = lax.fori_loop(
        *own, lambda w, c: apply(b_s, 0, u1_ref, 1, w, c, ((0, 0), (0, 1), (1, 1))), (zero,) * 3
    )
    halo(b_s, 0, u1_ref, 1, LOW + slab, first + slab >= width)
    halo(b_s, 0, u1_ref, 1, LOW + slab + 1, first + slab + 1 >= width)
    m3, m4 = lax.fori_loop(
        *own, lambda w, c: apply(u1_ref, 1, u2_ref, LOW, w, c, ((0, 1), (1, 1))), (zero,) * 2
    )
    halo(u1_ref, 1, u2_ref, LOW, LOW + slab, first + slab >= width)

    def last(w, carry):
        rows = [u2_ref[w - LOW, y] for y in range(width)] + [zero]
        terms = []
        for y in range(width):
            mid = rows[y]
            above = (rows[y + 1] + u2_ref[w + 1 - LOW, y]) + jnp.where(
                at_high, 0.0, pltpu.roll(mid, 127, 1)
            )
            terms.append(mid * (d_row(w, y) * mid - 2.0 * above))
        return carry + tree(terms)

    m5 = lax.fori_loop(*own, last, zero)
    column = lax.broadcasted_iota(jnp.int32, (128, 128), 1)
    half = lax.broadcasted_iota(jnp.int32, (128, 128), 0) // width
    packed = sh_ref[...]
    for k, moment in enumerate((m0, m1, m2, m3, m4, m5)):
        packed = packed + dot(moment, jnp.where(column == 2 * k + half, 1.0, 0.0))
    for peer in range(group):
        pay_ref[peer] = packed


def combine_kernel(
    slab, lines, width, group, share, flag_ref, pay_ref, v_ref, o_ref, u1_ref, u2_ref, cy_ref, cz_ref, out_ref, field_s
):
    chunks = out_ref.shape[0]
    if share:
        rows = share * lines
        for k in range(chunks):
            out_ref[k, slab * lines : slab * lines + rows, :] = v_ref[
                k, pl.ds(flag_ref[2] * rows + LOW * lines, rows), :
            ]
    total = pay_ref[0]
    for k in range(1, group):
        total = total + pay_ref[k]
    row = lax.broadcasted_iota(jnp.int32, (128, 128), 0)
    half = lax.broadcasted_iota(jnp.int32, (128, 128), 1) // width
    m = [dot(total, jnp.where(row == 2 * k + half, 1.0, 0.0)) for k in range(MOMENTS)]
    shift = dot(total, jnp.where(row == SHIFT_LANE, 1.0, 0.0))
    inv = 1.0 / m[0]
    mu = [None] + [m[k] * inv * (8.0**-k) for k in range(1, MOMENTS)]
    sigma = 0.25 * (shift + CENTER)
    k00 = mu[1] + sigma
    k01 = mu[2] + sigma * mu[1]
    k11 = mu[3] + sigma * mu[2]
    k02 = k11
    k12 = mu[4] + sigma * mu[3]
    k22 = mu[5] + sigma * mu[4]
    r0 = 1.0 / k00
    l10 = k01 * r0
    l20 = k02 * r0
    d1 = k11 - l10 * k01
    t = k12 - l20 * k01
    l21 = t / d1
    d2 = k22 - l20 * k02 - l21 * t
    z1 = mu[1] - l10
    z2 = mu[2] - l20 - l21 * z1
    y2 = z2 / d2
    y1 = z1 / d1 - l21 * y2
    y0 = r0 - l10 * y1 - l20 * y2
    c0 = -0.25 * y0
    c1 = (-0.25 / 8.0) * y1
    c2 = (-0.25 / 64.0) * y2

    def plane(x, carry):
        w = x + LOW
        for y in range(width):
            o = o_ref[w, y].astype(F32)
            b = o * v_ref[y // lines, pl.ds(w * lines + y % lines, 1), :]
            part = o * (c0 * b + (c1 * u1_ref[x + LOW - 1, y] + c2 * u2_ref[x, y]))
            field_s[8 * y : 8 * y + 8, :] = part[0:8] + part[8:16]
        planes = dot(dot(cy_ref[...], field_s[...]), cz_ref[...])
        for k in range(chunks):
            out_ref[k, pl.ds(x * lines, lines), :] = planes[k * lines : (k + 1) * lines]
        return carry

    lax.fori_loop(0, slab, plane, 0)


def gathered(got_ref, cx_ref, group):
    n = got_ref.shape[0]
    rows = cx_ref.shape[0] // group
    parts = []
    for j in range(group):
        parts.append(tree([got_ref[q * group + j, 0:rows, :] for q in range(n // group)]))
    return dot(cx_ref[...], jnp.concatenate(parts, axis=0))


def mapped_kernel(slab, lines, width, group, got_ref, cx_ref, mapped_ref, t_ref, pay_ref):
    n, size, _ = pay_ref.shape
    mapped = gathered(got_ref, cx_ref, group)
    mapped_ref[...] = mapped
    rounds = n // group
    rows = slab // rounds * lines
    for j in range(group):
        for q in range(rounds):
            at = (j * rounds + q) * rows
            t_ref[at : at + rows, :] = got_ref[q * group + j, slab * lines : slab * lines + rows, :]
    t = t_ref[...]
    sums = [jnp.sum(a * b, axis=0, keepdims=True) for a, b in ((t, t), (t, mapped), (mapped, mapped))]
    window = (slab + LOW + HIGH) * lines
    for k in range(n):
        start = (k % group) * slab * lines - LOW * lines
        low, high = max(start, 0), min(start + window, width * lines)
        pay_ref[k] = jnp.zeros((size, 128), F32)
        pay_ref[k, low - start : high - start, :] = mapped_ref[low:high, :]
        for i, s in enumerate(sums):
            pay_ref[k, size - 8 + i : size - 7 + i, :] = s


def second_kernel(group, got_ref, cx_ref, t_ref, mapped_ref, cs_ref, second_ref):
    again = gathered(got_ref, cx_ref, group)
    center, inverse = cs_ref[0:1], cs_ref[1:2]
    t = t_ref[...]
    first = (mapped_ref[...] - center * t) * inverse
    second_ref[...] = 2.0 * (again - center * first) * inverse - t


def turn(x):
    return pltpu.roll(x, 64, x.ndim - 1)


def gram_kernel(per, second_ref, other_ref, pay_ref):
    n, size, _ = pay_ref.shape
    a, b = second_ref[...], other_ref[...]
    a1, b1 = turn(a), turn(b)
    pairs = ((a, a), (a, a1), (a, b), (a, b1), (b, b), (b, b1))
    sums = [jnp.sum(p * q, axis=0, keepdims=True) for p, q in pairs]
    block = jnp.concatenate(sums + [jnp.zeros((8 - len(sums), 128), F32)], axis=0)
    for k in range(n):
        pay_ref[k, 0:per, :] = second_ref[k * per : (k + 1) * per, :]
        pay_ref[k, size - 8 : size, :] = block


def final_kernel(per, width, flag_ref, got_ref, other_ref, out_ref):
    n, size, _ = got_ref.shape
    total = tree([got_ref[k, size - 8 : size, :] for k in range(n)])
    total = dot(total, halves(8, width)) / float(width**3)
    swapped = turn(total)
    lane = lax.broadcasted_iota(jnp.int32, (1, 128), 1)
    in_first = lane < width
    is_low = jnp.zeros((1, 128), jnp.int32) + flag_ref[1] == 0

    def entry(k, t):
        here, there = total[k : k + 1], swapped[k : k + 1]
        return jnp.where(in_first, here, there) if t == 0 else jnp.where(in_first, there, here)

    aa = ((entry(0, 0), entry(1, 0)), (entry(1, 0), entry(0, 1)))
    bb = ((entry(4, 0), entry(5, 0)), (entry(5, 0), entry(4, 1)))
    ab = ((entry(2, 0), entry(3, 0)), (entry(3, 1), entry(2, 1)))
    m = [[None] * 4 for _ in range(4)]
    for i in range(2):
        for j in range(2):
            m[i][j] = jnp.where(is_low, aa[i][j], bb[i][j])
            m[2 + i][2 + j] = jnp.where(is_low, bb[i][j], aa[i][j])
            m[2 + j][i] = jnp.where(is_low, ab[i][j], ab[j][i])
    low = [[None] * 4 for _ in range(4)]
    inv = [[jnp.zeros((1, 128), F32)] * 4 for _ in range(4)]
    for j in range(4):
        pivot = m[j][j]
        for k in range(j):
            pivot = pivot - low[j][k] * low[j][k]
        inv[j][j] = 1.0 / jnp.sqrt(pivot)
        for i in range(j + 1, 4):
            value = m[i][j]
            for k in range(j):
                value = value - low[i][k] * low[j][k]
            low[i][j] = value * inv[j][j]
    for j in range(4):
        for i in range(j + 1, 4):
            value = low[i][j] * inv[j][j]
            for k in range(j + 1, i):
                value = value + low[i][k] * inv[k][j]
            inv[i][j] = -value * inv[i][i]

    def pick(i, j):
        return jnp.where(is_low, inv[i][j], inv[2 + i][(j + 2) % 4])

    c = [
        jnp.where(in_first, pick(0, a), pick(1, b)) for a, b in ((0, 1), (1, 0), (2, 3), (3, 2))
    ]
    for k in range(n):
        a, b = got_ref[k, 0:per, :], other_ref[k]
        out_ref[k] = (c[0] * a + c[1] * turn(a)) + (c[2] * b + c[3] * turn(b))


def vmem():
    return pl.BlockSpec(memory_space=pltpu.VMEM)


def smem():
    return pl.BlockSpec(memory_space=pltpu.SMEM)


def call(kernel, name, shapes, inputs, scratch=(), limit=4, in_smem=()):
    return pl.pallas_call(
        kernel,
        out_shape=shapes,
        in_specs=[smem() if k in in_smem else vmem() for k in range(len(inputs))],
        out_specs=jax.tree.map(lambda _: vmem(), shapes),
        scratch_shapes=scratch,
        compiler_params=pltpu.CompilerParams(vmem_limit_bytes=limit * MIB),
        name=name,
    )(*inputs)


def shape(*dims):
    return jax.ShapeDtypeStruct(dims, F32)


def up8(x):
    return -(-x // 8) * 8


def shards(n, cores, trials, orbitals, potential, coulomb, energies, frequencies, orbital_ids, freq_index):
    count, planes, cells = trials.shape
    held = orbitals.shape[0]
    width = coulomb.shape[1]
    lines = width // n
    group = ORBS // held
    slab = width // group
    window = slab + LOW + HIGH
    me = lax.axis_index("orb")
    core = lax.axis_index("trial")
    place = me % group
    pairs = cells // 128
    each = held // cores
    groups = [list(range(q * group, (q + 1) * group)) for q in range(n // group)]

    def swap(x):
        return lax.ppermute(x, "trial", [(k, (k + 1) % cores) for k in range(cores)])

    def exchange(x):
        return lax.all_to_all(x, "orb", split_axis=0, concat_axis=0, tiled=True)

    def exchange_group(x):
        return lax.all_to_all(
            x, "orb", split_axis=0, concat_axis=0, tiled=True, axis_index_groups=groups
        )

    mine = lax.dynamic_slice_in_dim(orbitals, core * each, each, 0).astype(F32)
    mine = mine.reshape(each, width * pairs, 128)
    sent = call(
        functools.partial(pack_kernel, slab, window, width, pairs),
        "pack_orbitals",
        shape(group, each * window * pairs, 128),
        (mine,),
        limit=8,
    )
    own_half = exchange_group(sent)
    own_half = own_half.reshape(ORBS // 2 * window * pairs, 128)
    shifts = orbital_shifts(orbital_ids, freq_index, energies, frequencies)
    shifts = jnp.where(core == 0, shifts, jnp.roll(shifts, -each))
    slot_rows = [(k // each) * (ORBS // 2) + place * each + k % each for k in range(held)]
    row = lax.broadcasted_iota(jnp.int32, (ORBS, 128), 0)
    lane = lax.broadcasted_iota(jnp.int32, (ORBS, 128), 1)
    shift_rows = sum(
        jnp.where((row == slot_rows[k]) & (lane == SHIFT_LANE), shifts[k], 0.0) for k in range(held)
    )

    rounds = n // group
    flags = jnp.stack([place * slab, core, me // group]).astype(jnp.int32)
    fields = jnp.concatenate([trials, potential[None]], axis=0).reshape(count + 1, planes * pairs, 128)
    blocks = [
        lax.ppermute(
            fields,
            "orb",
            [
                (j * rounds + k, (k + r) % rounds * group + j)
                for j in range(group)
                for k in range(rounds)
            ],
        )
        for r in range(rounds)
    ]
    slabs = call(
        functools.partial(slab_kernel, rounds),
        "slab",
        shape(count + 1, slab * pairs, 128),
        (flags, *blocks),
        limit=8,
        in_smem=(0,),
    )
    if planes >= HIGH and rounds == 2:
        last = me % rounds == rounds - 1
        edge = jnp.where(last, fields[:, (planes - HIGH) * pairs :], fields[:, : HIGH * pairs])
        first, other = (
            lax.ppermute(
                edge,
                "orb",
                [((j - 1) * rounds + 1, q * group + j) for j in range(1, group)]
                + [((j + 1) * rounds, (1 - q) * group + j) for j in range(group - 1)],
            )
            for q in range(rounds)
        )
        is_first = me // group == 0
        low = jnp.where(is_first, first, other)[:, (HIGH - LOW) * pairs :]
        high = jnp.where(is_first, other, first)
    else:
        low = lax.ppermute(
            slabs[:, (slab - LOW) * pairs :], "orb", [(i, i + 1) for i in range(n) if i % group < group - 1]
        )
        high = lax.ppermute(slabs[:, : HIGH * pairs], "orb", [(i, i - 1) for i in range(n) if i % group > 0])
    used = window * lines
    trial_window, diag_window = call(
        functools.partial(fields_kernel, slab, lines, pairs),
        "fields",
        (shape(n, used, 128), shape(n, used, 128)),
        (slabs, low, high),
        limit=8,
    )
    cx, cy, cz = call(
        functools.partial(factors_kernel, lines, width),
        "factors",
        (shape(width * lines, width * lines), shape(width, 8 * width), shape(128, 128)),
        (coulomb,),
    )
    trial_window, diag_window, cx, cy, cz, shift_rows, own_half = lax.optimization_barrier(
        (trial_window, diag_window, cx, cy, cz, shift_rows, own_half)
    )
    spread_orbitals = call(
        functools.partial(spread_kernel, window, pairs),
        "spread_orbitals",
        jax.ShapeDtypeStruct((window, width, ORBS, 128), jnp.bfloat16),
        (own_half, swap(own_half)),
        limit=4,
    )

    def response(fields):
        filtered = len(fields) == 2
        share = 0 if filtered else slab // rounds
        shapes = [
            shape(slab + 3, width, ORBS, 128), shape(slab + 1, width, ORBS, 128), shape(group, ORBS, 128),
        ]
        if filtered:
            shapes += [shape(n, used, 128), shape(8, 128)]
        made = call(
            functools.partial(krylov_kernel, slab, lines, width, group, filtered),
            "krylov",
            tuple(shapes),
            (flags, spread_orbitals, diag_window, shift_rows, *fields),
            scratch=[pltpu.VMEM((window, width, ORBS, 128), F32)],
            limit=14,
            in_smem=(0,),
        )
        u1, u2, pay = made[:3]
        v = made[3] if filtered else fields[0]
        part = call(
            functools.partial(combine_kernel, slab, lines, width, group, share),
            "combine",
            shape(n, up8((slab + share) * lines), 128),
            (flags, exchange_group(pay), v, spread_orbitals, u1, u2, cy, cz),
            scratch=[pltpu.VMEM((8 * width, 128), F32)],
            limit=4,
            in_smem=(0,),
        )
        return exchange(part), (made[4] if filtered else None)

    got, _ = response((trial_window,))
    mapped, trial_rows, pay = call(
        functools.partial(mapped_kernel, slab, lines, width, group),
        "mapped",
        (shape(width * lines, 128), shape(width * lines, 128), shape(n, up8(used) + 8, 128)),
        (got, cx),
    )
    got, scales = response((trial_window, exchange(pay)))
    second = call(
        functools.partial(second_kernel, group),
        "second",
        shape(width * lines, 128),
        (got, cx, trial_rows, mapped, scales),
    )
    per = planes * lines
    pay = call(functools.partial(gram_kernel, per), "gram", shape(n, up8(per) + 8, 128), (second, swap(second)))
    got = exchange(pay)
    result = call(
        functools.partial(final_kernel, per, width),
        "final",
        shape(n, per, 128),
        (flags, got, swap(got[:, :per])),
        in_smem=(0,),
    )
    result = result.reshape(n, planes, lines, count, width).transpose(3, 1, 0, 2, 4)
    return result.reshape(count, planes, cells)


def solution(mesh):
    n, cores = mesh.shape["orb"], mesh.shape["trial"]
    in_specs = (
        P("trial", "orb", None), P("orb", None, None), P("orb", None), P(), P(), P(), P("orb"), P("orb"),
    )
    return jax.shard_map(
        functools.partial(shards, n, cores),
        mesh=mesh, in_specs=in_specs, out_specs=P("trial", "orb", None), check_vma=False,
    )
```

```python
import functools
import jax
import jax.numpy as jnp
from jax import lax
from jax.experimental import pallas as pl
from jax.experimental.pallas import tpu as pltpu
from jax.sharding import PartitionSpec as P

LOW = 2
HIGH = 3
CENTER = 4.25
ORBS = 16
SHIFT_LANE = 12
MOMENTS = 6
HIGHEST = lax.Precision.HIGHEST
F32 = jnp.float32
MIB = 2**20


def dot(a, b):
    return jnp.dot(a, b, precision=HIGHEST, preferred_element_type=F32)


def halves(rows, width, value=1.0):
    a = lax.broadcasted_iota(jnp.int32, (128, 128), 0) // width
    b = lax.broadcasted_iota(jnp.int32, (128, 128), 1) // width
    return jnp.where(a == b, 1.0, 0.0)


def tree(terms):
    while len(terms) > 1:
        odd = [terms[-1]] if len(terms) % 2 else []
        terms = [a + b for a, b in zip(terms[::2], terms[1::2])] + odd
    return terms[0]


def orbital_shifts(orbital_ids, freq_index, energies, frequencies):
    energy_slots = lax.broadcasted_iota(jnp.int32, (1, energies.shape[0]), 1)
    picked_energy = jnp.sum(
        jnp.where(orbital_ids[:, None] == energy_slots, energies[None, :], 0.0), axis=1
    )
    freq_slots = lax.broadcasted_iota(jnp.int32, (1, frequencies.shape[0]), 1)
    picked_freq = jnp.sum(
        jnp.where(freq_index[:, None] == freq_slots, frequencies[None, :], 0.0), axis=1
    )
    return picked_freq - picked_energy


def spread_kernel(window, pairs, own_ref, other_ref, dst_ref):
    half = ORBS // 2
    rows = window * pairs
    first_half = lax.broadcasted_iota(jnp.int32, (ORBS, 128), 1) < 64

    def body(w, carry):
        for i in range(pairs):
            at = pl.ds(w * pairs + i, half, stride=rows)
            pair = jnp.concatenate([own_ref[at, :], other_ref[at, :]], axis=0)
            turned = pltpu.roll(pair, 64, 1)
            dst_ref[w, 2 * i] = jnp.where(first_half, pair, turned).astype(jnp.bfloat16)
            dst_ref[w, 2 * i + 1] = jnp.where(first_half, turned, pair).astype(jnp.bfloat16)
        return carry

    lax.fori_loop(0, window, body, 0)


def pack_kernel(slab, window, width, pairs, src_ref, dst_ref):
    each = src_ref.shape[0]
    size = window * pairs
    for j in range(dst_ref.shape[0]):
        start = (j * slab - LOW) * pairs
        low, high = max(start, 0), min(start + size, width * pairs)
        for e in range(each):
            if low > start:
                dst_ref[j, e * size : e * size + low - start, :] = jnp.zeros((low - start, 128), F32)
            if high < start + size:
                dst_ref[j, e * size + high - start : (e + 1) * size, :] = jnp.zeros(
                    (start + size - high, 128), F32
                )
            dst_ref[j, e * size + low - start : e * size + high - start, :] = src_ref[e, low:high, :]


def equal(rows, columns, left, right):
    a = lax.broadcasted_iota(jnp.int32, (rows, columns), 0)
    b = lax.broadcasted_iota(jnp.int32, (rows, columns), 1)
    return left(a) == right(b)


def factors_kernel(lines, width, c_ref, cx_ref, cz_ref):
    size = width * lines
    pick = jnp.where(equal(size, width, lambda a: a // lines, lambda b: b), 1.0, 0.0)
    turned = jnp.where(equal(width, size, lambda a: a, lambda b: b // lines), 1.0, 0.0)
    same = equal(size, size, lambda a: a % lines, lambda b: b % lines)
    cx_ref[...] = jnp.where(same, dot(dot(pick, c_ref[0]), turned), 0.0)
    pick = jnp.where(equal(128, width, lambda a: a % width, lambda b: b), 1.0, 0.0)
    turned = jnp.where(equal(width, 128, lambda a: a, lambda b: b % width), 1.0, 0.0)
    same = equal(128, 128, lambda a: a // width, lambda b: b // width)
    cz_ref[...] = jnp.where(same, dot(dot(pick, c_ref[2].T), turned), 0.0)


def slab_kernel(rounds, flag_ref, *refs):
    dst_ref = refs[rounds]
    rows = refs[0].shape[1]
    for r in range(rounds):
        k = lax.rem(flag_ref[2] - r + rounds, rounds)
        dst_ref[:, pl.ds(pl.multiple_of(k * rows, 8), rows), :] = refs[r][...]


def fields_kernel(slab, lines, pairs, slab_ref, low_ref, high_ref, v_ref, d_ref):
    first_half = lax.broadcasted_iota(jnp.int32, (8, 128), 1) < 64

    def both(a, b):
        return jnp.where(first_half, a, turn(b)), jnp.where(first_half, turn(a), b)

    for w in range(slab + LOW + HIGH):
        if w < LOW:
            ref, at = low_ref, w
        elif w < LOW + slab:
            ref, at = slab_ref, w - LOW
        else:
            ref, at = high_ref, w - LOW - slab
        for rb in range(pairs // 8):
            rows = slice(at * pairs + 8 * rb, at * pairs + 8 * rb + 8)
            v = both(ref[0, rows, :], ref[1, rows, :])
            diag = 2.0 * (3.0 - CENTER + ref[2, rows, :])
            d = both(diag, diag)
            for i in range(8):
                for h in range(2):
                    y = 2 * (8 * rb + i) + h
                    row = w * lines + y % lines
                    v_ref[y // lines, row : row + 1, :] = v[h][i : i + 1]
                    d_ref[y // lines, row : row + 1, :] = d[h][i : i + 1]


def krylov_kernel(slab, lines, width, group, filtered, *refs):
    flag_ref, o_ref, d_ref, sh_ref, t_ref = refs[:5]
    if filtered:
        m_ref, u1_ref, u2_ref, pay_ref, v_ref, cs_ref, b_s = refs[5:]
    else:
        u1_ref, u2_ref, pay_ref, b_s = refs[5:]
        v_ref = t_ref
    window = slab + LOW + HIGH
    lane = lax.broadcasted_iota(jnp.int32, (ORBS, 128), 1)
    at_low = lane % width == 0
    at_high = lane % width == width - 1
    zero = jnp.zeros((ORBS, 128), F32)
    n = t_ref.shape[0]

    if filtered:
        base = window * lines
        total = m_ref[0, base : base + 3, :]
        for k in range(1, n):
            total = total + m_ref[k, base : base + 3, :]
        total = jnp.concatenate([total, jnp.zeros((5, 128), F32)], axis=0)
        total = dot(total, halves(8, width))
        center = total[1:2] / total[0:1]
        inverse = 1.0 / jnp.sqrt(total[2:3] / total[0:1])
        cs_ref[0:1] = center
        cs_ref[1:2] = inverse
        used = v_ref.shape[1]
        for k in range(n):
            v_ref[k] = (m_ref[k, 0:used, :] - center * t_ref[k, 0:used, :]) * inverse

    def v_row(w, y):
        return v_ref[y // lines, pl.ds(w * lines + y % lines, 1), :]

    def d_row(w, y):
        return d_ref[y // lines, pl.ds(w * lines + y % lines, 1), :]

    def products(w, carry):
        for y in range(width):
            b_s[w, y] = o_ref[w, y].astype(F32) * v_row(w, y)
        return carry

    lax.fori_loop(0, window, products, 0)

    def apply(src, src_at, dst, dst_at, w, carry, pairs):
        rows = [zero] + [src[w - src_at, y] for y in range(width)] + [zero]
        terms = [[] for _ in carry]
        for y in range(width):
            mid = rows[y + 1]
            around = (rows[y] + rows[y + 2]) + (src[w - 1 - src_at, y] + src[w + 1 - src_at, y])
            around = around + (
                jnp.where(at_low, 0.0, pltpu.roll(mid, 1, 1))
                + jnp.where(at_high, 0.0, pltpu.roll(mid, 127, 1))
            )
            new = d_row(w, y) * mid - around
            dst[w - dst_at, y] = new
            both = (mid, new)
            for list_at, (a, b) in zip(terms, pairs):
                list_at.append(both[a] * both[b])
        return tuple(old + tree(t) for old, t in zip(carry, terms))

    def halo(src, src_at, dst, dst_at, w, outside):
        @pl.when(outside)
        def _():
            dst[w - dst_at] = jnp.zeros((width, ORBS, 128), F32)

        @pl.when(jnp.logical_not(outside))
        def _():
            apply(src, src_at, dst, dst_at, w, (), ())

    first = flag_ref[0]
    own = (LOW, LOW + slab)
    halo(b_s, 0, u1_ref, 1, LOW - 1, first < 1)
    m0, m1, m2 = lax.fori_loop(
        *own,
        lambda w, c: apply(b_s, 0, u1_ref, 1, w, c, ((0, 0), (0, 1), (1, 1))), (zero,) * 3,
        unroll=True,
    )
    halo(b_s, 0, u1_ref, 1, LOW + slab, first + slab >= width)
    halo(b_s, 0, u1_ref, 1, LOW + slab + 1, first + slab + 1 >= width)
    m3, m4 = lax.fori_loop(
        *own,
        lambda w, c: apply(u1_ref, 1, u2_ref, LOW, w, c, ((0, 1), (1, 1))), (zero,) * 2,
        unroll=True,
    )
    halo(u1_ref, 1, u2_ref, LOW, LOW + slab, first + slab >= width)

    def last(w, carry):
        rows = [u2_ref[w - LOW, y] for y in range(width)] + [zero]
        terms = []
        for y in range(width):
            mid = rows[y]
            above = (rows[y + 1] + u2_ref[w + 1 - LOW, y]) + jnp.where(
                at_high, 0.0, pltpu.roll(mid, 127, 1)
            )
            terms.append(mid * (d_row(w, y) * mid - 2.0 * above))
        return carry + tree(terms)

    m5 = lax.fori_loop(*own, last, zero, unroll=True)
    column = lax.broadcasted_iota(jnp.int32, (128, 128), 1)
    half = lax.broadcasted_iota(jnp.int32, (128, 128), 0) // width
    packed = sh_ref[...]
    for k, moment in enumerate((m0, m1, m2, m3, m4, m5)):
        packed = packed + dot(moment, jnp.where(column == 2 * k + half, 1.0, 0.0))
    for peer in range(group):
        pay_ref[peer] = packed


def combine_kernel(
    slab, lines, width, group, share, flag_ref, pay_ref, v_ref, o_ref, u1_ref, u2_ref, cy_ref, cz_ref, out_ref, field_s
):
    chunks = out_ref.shape[0]
    if share:
        rows = share * lines
        for k in range(chunks):
            out_ref[k, slab * lines : slab * lines + rows, :] = v_ref[
                k, pl.ds(flag_ref[2] * rows + LOW * lines, rows), :
            ]
    total = pay_ref[0]
    for k in range(1, group):
        total = total + pay_ref[k]
    row = lax.broadcasted_iota(jnp.int32, (128, 128), 0)
    half = lax.broadcasted_iota(jnp.int32, (128, 128), 1) // width
    m = [dot(total, jnp.where(row == 2 * k + half, 1.0, 0.0)) for k in range(MOMENTS)]
    shift = dot(total, jnp.where(row == SHIFT_LANE, 1.0, 0.0))
    inv = 1.0 / m[0]
    mu = [None] + [m[k] * inv * (8.0**-k) for k in range(1, MOMENTS)]
    sigma = 0.25 * (shift + CENTER)
    k00 = mu[1] + sigma
    k01 = mu[2] + sigma * mu[1]
    k11 = mu[3] + sigma * mu[2]
    k02 = k11
    k12 = mu[4] + sigma * mu[3]
    k22 = mu[5] + sigma * mu[4]
    r0 = 1.0 / k00
    l10 = k01 * r0
    l20 = k02 * r0
    d1 = k11 - l10 * k01
    t = k12 - l20 * k01
    l21 = t / d1
    d2 = k22 - l20 * k02 - l21 * t
    z1 = mu[1] - l10
    z2 = mu[2] - l20 - l21 * z1
    y2 = z2 / d2
    y1 = z1 / d1 - l21 * y2
    y0 = r0 - l10 * y1 - l20 * y2
    c0 = -0.25 * y0
    c1 = (-0.25 / 8.0) * y1
    c2 = (-0.25 / 64.0) * y2

    sublane = lax.broadcasted_iota(jnp.int32, (8, 128), 0)
    takes = [(sublane // step) % 2 == 0 for step in (1, 2, 4)]

    def merge(values):
        for take, step in zip(takes, (1, 2, 4)):
            values = [
                jnp.where(take, a, b) + pltpu.roll(jnp.where(take, b, a), step, 0)
                for a, b in zip(values[::2], values[1::2])
            ]
        return values[0]

    def plane(x, carry):
        w = x + LOW
        for y0 in range(0, width, 8):
            values = []
            for y in range(y0, y0 + 8):
                o = o_ref[w, y].astype(F32)
                b = o * v_ref[y // lines, pl.ds(w * lines + y % lines, 1), :]
                part = o * (c0 * b + (c1 * u1_ref[x + LOW - 1, y] + c2 * u2_ref[x, y]))
                values.append(part[0:8] + part[8:16])
            field_s[pl.ds(pl.multiple_of(x * width + y0, 8), 8), :] = merge(values)
        return carry

    lax.fori_loop(0, slab, plane, 0)
    turned = dot(field_s[...], cz_ref[...])
    turned = jnp.concatenate([turned[x * width : (x + 1) * width] for x in range(slab)], axis=1)
    planes = dot(cy_ref[...], turned)
    for x in range(slab):
        for k in range(chunks):
            out_ref[k, x * lines : (x + 1) * lines, :] = planes[
                k * lines : (k + 1) * lines, x * 128 : (x + 1) * 128
            ]


def gathered(got_ref, cx_ref, group):
    n = got_ref.shape[0]
    rows = cx_ref.shape[0] // group
    parts = []
    for j in range(group):
        parts.append(tree([got_ref[q * group + j, 0:rows, :] for q in range(n // group)]))
    return dot(cx_ref[...], jnp.concatenate(parts, axis=0))


def mapped_kernel(slab, lines, width, group, got_ref, cx_ref, mapped_ref, t_ref, pay_ref):
    n, size, _ = pay_ref.shape
    mapped = gathered(got_ref, cx_ref, group)
    mapped_ref[...] = mapped
    rounds = n // group
    rows = slab // rounds * lines
    for j in range(group):
        for q in range(rounds):
            at = (j * rounds + q) * rows
            t_ref[at : at + rows, :] = got_ref[q * group + j, slab * lines : slab * lines + rows, :]
    t = t_ref[...]
    sums = [jnp.sum(a * b, axis=0, keepdims=True) for a, b in ((t, t), (t, mapped), (mapped, mapped))]
    window = (slab + LOW + HIGH) * lines
    for k in range(n):
        start = (k % group) * slab * lines - LOW * lines
        low, high = max(start, 0), min(start + window, width * lines)
        pay_ref[k] = jnp.zeros((size, 128), F32)
        pay_ref[k, low - start : high - start, :] = mapped_ref[low:high, :]
        for i, s in enumerate(sums):
            pay_ref[k, window + i : window + i + 1, :] = s


def second_kernel(group, got_ref, cx_ref, t_ref, mapped_ref, cs_ref, second_ref):
    again = gathered(got_ref, cx_ref, group)
    center, inverse = cs_ref[0:1], cs_ref[1:2]
    t = t_ref[...]
    first = (mapped_ref[...] - center * t) * inverse
    second_ref[...] = 2.0 * (again - center * first) * inverse - t


def turn(x):
    return pltpu.roll(x, 64, x.ndim - 1)


def gram_kernel(per, second_ref, other_ref, pay_ref):
    n, size, _ = pay_ref.shape
    a, b = second_ref[...], other_ref[...]
    a1, b1 = turn(a), turn(b)
    pairs = ((a, a), (a, a1), (a, b), (a, b1), (b, b), (b, b1))
    sums = [jnp.sum(p * q, axis=0, keepdims=True) for p, q in pairs]
    block = jnp.concatenate(sums + [jnp.zeros((8 - len(sums), 128), F32)], axis=0)
    for k in range(n):
        pay_ref[k, 0:per, :] = second_ref[k * per : (k + 1) * per, :]
        pay_ref[k, size - 8 : size, :] = block


def final_kernel(per, width, flag_ref, got_ref, other_ref, out_ref):
    n, size, _ = got_ref.shape
    total = tree([got_ref[k, size - 8 : size, :] for k in range(n)])
    total = dot(total, halves(8, width)) / float(width**3)
    swapped = turn(total)
    lane = lax.broadcasted_iota(jnp.int32, (1, 128), 1)
    in_first = lane < width
    is_low = jnp.zeros((1, 128), jnp.int32) + flag_ref[1] == 0

    def entry(k, t):
        here, there = total[k : k + 1], swapped[k : k + 1]
        return jnp.where(in_first, here, there) if t == 0 else jnp.where(in_first, there, here)

    aa = ((entry(0, 0), entry(1, 0)), (entry(1, 0), entry(0, 1)))
    bb = ((entry(4, 0), entry(5, 0)), (entry(5, 0), entry(4, 1)))
    ab = ((entry(2, 0), entry(3, 0)), (entry(3, 1), entry(2, 1)))
    m = [[None] * 4 for _ in range(4)]
    for i in range(2):
        for j in range(2):
            m[i][j] = jnp.where(is_low, aa[i][j], bb[i][j])
            m[2 + i][2 + j] = jnp.where(is_low, bb[i][j], aa[i][j])
            m[2 + j][i] = jnp.where(is_low, ab[i][j], ab[j][i])
    low = [[None] * 4 for _ in range(4)]
    inv = [[jnp.zeros((1, 128), F32)] * 4 for _ in range(4)]
    for j in range(4):
        pivot = m[j][j]
        for k in range(j):
            pivot = pivot - low[j][k] * low[j][k]
        inv[j][j] = 1.0 / jnp.sqrt(pivot)
        for i in range(j + 1, 4):
            value = m[i][j]
            for k in range(j):
                value = value - low[i][k] * low[j][k]
            low[i][j] = value * inv[j][j]
    for j in range(4):
        for i in range(j + 1, 4):
            value = low[i][j] * inv[j][j]
            for k in range(j + 1, i):
                value = value + low[i][k] * inv[k][j]
            inv[i][j] = -value * inv[i][i]

    def pick(i, j):
        return jnp.where(is_low, inv[i][j], inv[2 + i][(j + 2) % 4])

    c = [
        jnp.where(in_first, pick(0, a), pick(1, b)) for a, b in ((0, 1), (1, 0), (2, 3), (3, 2))
    ]
    for k in range(n):
        a, b = got_ref[k, 0:per, :], other_ref[k]
        out_ref[k] = (c[0] * a + c[1] * turn(a)) + (c[2] * b + c[3] * turn(b))


def vmem():
    return pl.BlockSpec(memory_space=pltpu.VMEM)


def smem():
    return pl.BlockSpec(memory_space=pltpu.SMEM)


def call(kernel, name, shapes, inputs, scratch=(), limit=4, in_smem=()):
    return pl.pallas_call(
        kernel,
        out_shape=shapes,
        in_specs=[smem() if k in in_smem else vmem() for k in range(len(inputs))],
        out_specs=jax.tree.map(lambda _: vmem(), shapes),
        scratch_shapes=scratch,
        compiler_params=pltpu.CompilerParams(vmem_limit_bytes=limit * MIB),
        name=name,
    )(*inputs)


def shape(*dims):
    return jax.ShapeDtypeStruct(dims, F32)


def up8(x):
    return -(-x // 8) * 8


def shards(n, cores, trials, orbitals, potential, coulomb, energies, frequencies, orbital_ids, freq_index):
    count, planes, cells = trials.shape
    held = orbitals.shape[0]
    width = coulomb.shape[1]
    lines = width // n
    group = ORBS // held
    slab = width // group
    window = slab + LOW + HIGH
    me = lax.axis_index("orb")
    core = lax.axis_index("trial")
    place = me % group
    pairs = cells // 128
    each = held // cores
    groups = [list(range(q * group, (q + 1) * group)) for q in range(n // group)]

    def swap(x):
        return lax.ppermute(x, "trial", [(k, (k + 1) % cores) for k in range(cores)])

    def exchange(x):
        return lax.all_to_all(x, "orb", split_axis=0, concat_axis=0, tiled=True)

    def exchange_group(x):
        return lax.all_to_all(
            x, "orb", split_axis=0, concat_axis=0, tiled=True, axis_index_groups=groups
        )

    mine = lax.dynamic_slice_in_dim(orbitals, core * each, each, 0).astype(F32)
    mine = mine.reshape(each, width * pairs, 128)
    sent = call(
        functools.partial(pack_kernel, slab, window, width, pairs),
        "pack_orbitals",
        shape(group, each * window * pairs, 128),
        (mine,),
        limit=8,
    )
    own_half = exchange_group(sent)
    own_half = own_half.reshape(ORBS // 2 * window * pairs, 128)
    shifts = orbital_shifts(orbital_ids, freq_index, energies, frequencies)
    shifts = jnp.where(core == 0, shifts, jnp.roll(shifts, -each))
    slot_rows = [(k // each) * (ORBS // 2) + place * each + k % each for k in range(held)]
    row = lax.broadcasted_iota(jnp.int32, (ORBS, 128), 0)
    lane = lax.broadcasted_iota(jnp.int32, (ORBS, 128), 1)
    shift_rows = sum(
        jnp.where((row == slot_rows[k]) & (lane == SHIFT_LANE), shifts[k], 0.0) for k in range(held)
    )

    rounds = n // group
    flags = jnp.stack([place * slab, core, me // group]).astype(jnp.int32)
    fields = jnp.concatenate([trials, potential[None]], axis=0).reshape(count + 1, planes * pairs, 128)
    blocks = [
        lax.ppermute(
            fields,
            "orb",
            [
                (j * rounds + k, (k + r) % rounds * group + j)
                for j in range(group)
                for k in range(rounds)
            ],
        )
        for r in range(rounds)
    ]
    slabs = call(
        functools.partial(slab_kernel, rounds),
        "slab",
        shape(count + 1, slab * pairs, 128),
        (flags, *blocks),
        limit=8,
        in_smem=(0,),
    )
    if planes >= HIGH and rounds == 2:
        last = me % rounds == rounds - 1
        edge = jnp.where(last, fields[:, (planes - HIGH) * pairs :], fields[:, : HIGH * pairs])
        first, other = (
            lax.ppermute(
                edge,
                "orb",
                [((j - 1) * rounds + 1, q * group + j) for j in range(1, group)]
                + [((j + 1) * rounds, (1 - q) * group + j) for j in range(group - 1)],
            )
            for q in range(rounds)
        )
        is_first = me // group == 0
        low = jnp.where(is_first, first, other)[:, (HIGH - LOW) * pairs :]
        high = jnp.where(is_first, other, first)
    else:
        low = lax.ppermute(
            slabs[:, (slab - LOW) * pairs :], "orb", [(i, i + 1) for i in range(n) if i % group < group - 1]
        )
        high = lax.ppermute(slabs[:, : HIGH * pairs], "orb", [(i, i - 1) for i in range(n) if i % group > 0])
    used = window * lines
    trial_window, diag_window = call(
        functools.partial(fields_kernel, slab, lines, pairs),
        "fields",
        (shape(n, used, 128), shape(n, used, 128)),
        (slabs, low, high),
        limit=8,
    )
    cy = coulomb[1]
    cx, cz = call(
        functools.partial(factors_kernel, lines, width),
        "factors",
        (shape(width * lines, width * lines), shape(128, 128)),
        (coulomb,),
    )
    trial_window, diag_window, cx, cy, cz, shift_rows, own_half = lax.optimization_barrier(
        (trial_window, diag_window, cx, cy, cz, shift_rows, own_half)
    )
    spread_orbitals = call(
        functools.partial(spread_kernel, window, pairs),
        "spread_orbitals",
        jax.ShapeDtypeStruct((window, width, ORBS, 128), jnp.bfloat16),
        (own_half, swap(own_half)),
        limit=4,
    )

    def response(fields):
        filtered = len(fields) == 2
        share = 0 if filtered else slab // rounds
        shapes = [
            shape(slab + 3, width, ORBS, 128), shape(slab + 1, width, ORBS, 128), shape(group, ORBS, 128),
        ]
        if filtered:
            shapes += [shape(n, used, 128), shape(8, 128)]
        made = call(
            functools.partial(krylov_kernel, slab, lines, width, group, filtered),
            "krylov",
            tuple(shapes),
            (flags, spread_orbitals, diag_window, shift_rows, *fields),
            scratch=[pltpu.VMEM((window, width, ORBS, 128), F32)],
            limit=14,
            in_smem=(0,),
        )
        u1, u2, pay = made[:3]
        v = made[3] if filtered else fields[0]
        part = call(
            functools.partial(combine_kernel, slab, lines, width, group, share),
            "combine",
            shape(n, up8((slab + share) * lines), 128),
            (flags, exchange_group(pay), v, spread_orbitals, u1, u2, cy, cz),
            scratch=[pltpu.VMEM((slab * width, 128), F32)],
            limit=4,
            in_smem=(0,),
        )
        return exchange(part), (made[4] if filtered else None)

    got, _ = response((trial_window,))
    mapped, trial_rows, pay = call(
        functools.partial(mapped_kernel, slab, lines, width, group),
        "mapped",
        (shape(width * lines, 128), shape(width * lines, 128), shape(n, up8(used + 3), 128)),
        (got, cx),
    )
    got, scales = response((trial_window, exchange(pay)))
    second = call(
        functools.partial(second_kernel, group),
        "second",
        shape(width * lines, 128),
        (got, cx, trial_rows, mapped, scales),
    )
    per = planes * lines
    pay = call(functools.partial(gram_kernel, per), "gram", shape(n, up8(per) + 8, 128), (second, swap(second)))
    got = exchange(pay)
    result = call(
        functools.partial(final_kernel, per, width),
        "final",
        shape(n, per, 128),
        (flags, got, swap(got[:, :per])),
        in_smem=(0,),
    )
    result = result.reshape(n, planes, lines, count, width).transpose(3, 1, 0, 2, 4)
    return result.reshape(count, planes, cells)


def solution(mesh):
    n, cores = mesh.shape["orb"], mesh.shape["trial"]
    in_specs = (
        P("trial", "orb", None), P("orb", None, None), P("orb", None), P(), P(), P(), P("orb"), P("orb"),
    )
    return jax.shard_map(
        functools.partial(shards, n, cores),
        mesh=mesh, in_specs=in_specs, out_specs=P("trial", "orb", None), check_vma=False,
    )
```

```python
import functools
import jax
import jax.numpy as jnp
from jax import lax
from jax.experimental import pallas as pl
from jax.experimental.pallas import tpu as pltpu
from jax.sharding import PartitionSpec as P

LOW = 2
HIGH = 3
CENTER = 4.25
ORBS = 16
HALF = 8
SHIFT_LANE = 12
MOMENTS = 6
HIGHEST = lax.Precision.HIGHEST
F32 = jnp.float32
MIB = 2**20


def dot(a, b):
    return jnp.dot(a, b, precision=HIGHEST, preferred_element_type=F32)


def halves(rows, width, value=1.0):
    a = lax.broadcasted_iota(jnp.int32, (128, 128), 0) // width
    b = lax.broadcasted_iota(jnp.int32, (128, 128), 1) // width
    return jnp.where(a == b, 1.0, 0.0)


def tree(terms):
    while len(terms) > 1:
        odd = [terms[-1]] if len(terms) % 2 else []
        terms = [a + b for a, b in zip(terms[::2], terms[1::2])] + odd
    return terms[0]


def orbital_shifts(orbital_ids, freq_index, energies, frequencies):
    energy_slots = lax.broadcasted_iota(jnp.int32, (1, energies.shape[0]), 1)
    picked_energy = jnp.sum(
        jnp.where(orbital_ids[:, None] == energy_slots, energies[None, :], 0.0), axis=1
    )
    freq_slots = lax.broadcasted_iota(jnp.int32, (1, frequencies.shape[0]), 1)
    picked_freq = jnp.sum(
        jnp.where(freq_index[:, None] == freq_slots, frequencies[None, :], 0.0), axis=1
    )
    return picked_freq - picked_energy


def spread_kernel(window, pairs, src_ref, dst_ref):
    rows = window * pairs
    first_half = lax.broadcasted_iota(jnp.int32, (HALF, 128), 1) < 64

    def body(w, carry):
        for i in range(pairs):
            pair = src_ref[pl.ds(w * pairs + i, HALF, stride=rows), :]
            turned = pltpu.roll(pair, 64, 1)
            dst_ref[w, 2 * i] = jnp.where(first_half, pair, turned)
            dst_ref[w, 2 * i + 1] = jnp.where(first_half, turned, pair)
        return carry

    lax.fori_loop(0, window, body, 0)


def pack_kernel(slab, window, width, pairs, src_ref, dst_ref):
    each = src_ref.shape[0]
    size = window * pairs
    for j in range(dst_ref.shape[0]):
        start = (j * slab - LOW) * pairs
        low, high = max(start, 0), min(start + size, width * pairs)
        for e in range(each):
            if low > start:
                dst_ref[j, e * size : e * size + low - start, :] = jnp.zeros((low - start, 128), F32)
            if high < start + size:
                dst_ref[j, e * size + high - start : (e + 1) * size, :] = jnp.zeros(
                    (start + size - high, 128), F32
                )
            dst_ref[j, e * size + low - start : e * size + high - start, :] = src_ref[e, low:high, :]


def equal(rows, columns, left, right):
    a = lax.broadcasted_iota(jnp.int32, (rows, columns), 0)
    b = lax.broadcasted_iota(jnp.int32, (rows, columns), 1)
    return left(a) == right(b)


def factors_kernel(lines, width, c_ref, cx_ref, cz_ref):
    size = width * lines
    pick = jnp.where(equal(size, width, lambda a: a // lines, lambda b: b), 1.0, 0.0)
    turned = jnp.where(equal(width, size, lambda a: a, lambda b: b // lines), 1.0, 0.0)
    same = equal(size, size, lambda a: a % lines, lambda b: b % lines)
    cx_ref[...] = jnp.where(same, dot(dot(pick, c_ref[0]), turned), 0.0)
    pick = jnp.where(equal(128, width, lambda a: a % width, lambda b: b), 1.0, 0.0)
    turned = jnp.where(equal(width, 128, lambda a: a, lambda b: b % width), 1.0, 0.0)
    same = equal(128, 128, lambda a: a // width, lambda b: b // width)
    cz_ref[...] = jnp.where(same, dot(dot(pick, c_ref[2].T), turned), 0.0)


def slab_kernel(rounds, flag_ref, *refs):
    dst_ref = refs[rounds]
    rows = refs[0].shape[1]
    for r in range(rounds):
        k = lax.rem(flag_ref[2] - r + rounds, rounds)
        dst_ref[:, pl.ds(pl.multiple_of(k * rows, 8), rows), :] = refs[r][...]


def fields_kernel(slab, lines, pairs, slab_ref, low_ref, high_ref, v_ref, d_ref):
    first_half = lax.broadcasted_iota(jnp.int32, (8, 128), 1) < 64

    def both(a, b):
        return jnp.where(first_half, a, turn(b)), jnp.where(first_half, turn(a), b)

    for w in range(slab + LOW + HIGH):
        if w < LOW:
            ref, at = low_ref, w
        elif w < LOW + slab:
            ref, at = slab_ref, w - LOW
        else:
            ref, at = high_ref, w - LOW - slab
        for rb in range(pairs // 8):
            rows = slice(at * pairs + 8 * rb, at * pairs + 8 * rb + 8)
            v = both(ref[0, rows, :], ref[1, rows, :])
            diag = 2.0 * (3.0 - CENTER + ref[2, rows, :])
            d = both(diag, diag)
            for i in range(8):
                for h in range(2):
                    y = 2 * (8 * rb + i) + h
                    row = w * lines + y % lines
                    v_ref[y // lines, row : row + 1, :] = v[h][i : i + 1]
                    d_ref[y // lines, row : row + 1, :] = d[h][i : i + 1]


def krylov_kernel(slab, lines, width, group, filtered, parts, before, *refs):
    refs = list(refs)
    take = lambda k: [refs.pop(0) for _ in range(k)]
    flag_ref, d_ref, sh_ref, t_ref = take(4)
    (m_ref,) = take(1) if filtered else (None,)
    packed_refs = take(before)
    o_refs = take(len(parts))
    u_refs = [take(2) for _ in parts]
    (pay_ref,) = take(1)
    v_ref, cs_ref = take(2) if filtered else (t_ref, None)
    (b_s,) = refs
    window = slab + LOW + HIGH
    lane = lax.broadcasted_iota(jnp.int32, (HALF, 128), 1)
    at_low = lane % width == 0
    at_high = lane % width == width - 1
    zero = jnp.zeros((HALF, 128), F32)
    n = t_ref.shape[0]

    if filtered:
        base = window * lines
        total = m_ref[0, base : base + 3, :]
        for k in range(1, n):
            total = total + m_ref[k, base : base + 3, :]
        total = jnp.concatenate([total, jnp.zeros((5, 128), F32)], axis=0)
        total = dot(total, halves(8, width))
        center = total[1:2] / total[0:1]
        inverse = 1.0 / jnp.sqrt(total[2:3] / total[0:1])
        cs_ref[0:1] = center
        cs_ref[1:2] = inverse
        used = v_ref.shape[1]
        for k in range(n):
            v_ref[k] = (m_ref[k, 0:used, :] - center * t_ref[k, 0:used, :]) * inverse

    def v_row(w, y):
        return v_ref[y // lines, pl.ds(w * lines + y % lines, 1), :]

    def d_row(w, y):
        return d_ref[y // lines, pl.ds(w * lines + y % lines, 1), :]

    b_refs = [b_s.at[k] for k in range(len(parts))]
    u1_refs, u2_refs = zip(*u_refs)

    def products(w, carry):
        for y in range(width):
            v = v_row(w, y)
            for b_ref, o_ref in zip(b_refs, o_refs):
                b_ref[w, y] = o_ref[w, y] * v
        return carry

    def apply(srcs, src_at, dsts, dst_at, w, carry, pairs, keep=None):
        fields = [[zero] + [src[w - src_at, y] for y in range(width)] + [zero] for src in srcs]
        terms = [[] for _ in srcs for _ in pairs]
        for y in range(width):
            diag = d_row(w, y)
            for k, (rows, src, dst) in enumerate(zip(fields, srcs, dsts)):
                mid = rows[y + 1]
                around = (rows[y] + rows[y + 2]) + (src[w - 1 - src_at, y] + src[w + 1 - src_at, y])
                around = around + (
                    jnp.where(at_low, 0.0, pltpu.roll(mid, 1, 1))
                    + jnp.where(at_high, 0.0, pltpu.roll(mid, 127, 1))
                )
                new = diag * mid - around
                if keep is not None:
                    new = new * keep
                dst[w - dst_at, y] = new
                both = (mid, new)
                for i, (a, b) in enumerate(pairs):
                    terms[k * len(pairs) + i].append(both[a] * both[b])
        return tuple(old + tree(t) for old, t in zip(carry, terms))

    def last(w, carry):
        fields = [[u2_ref[w - LOW, y] for y in range(width)] + [zero] for u2_ref in u2_refs]
        terms = [[] for _ in fields]
        for y in range(width):
            diag = d_row(w, y)
            for k, (rows, u2_ref) in enumerate(zip(fields, u2_refs)):
                mid = rows[y]
                above = (rows[y + 1] + u2_ref[w + 1 - LOW, y]) + jnp.where(
                    at_high, 0.0, pltpu.roll(mid, 127, 1)
                )
                terms[k].append(mid * (diag * mid - 2.0 * above))
        return tuple(old + tree(t) for old, t in zip(carry, terms))

    first = flag_ref[0]
    own, top = (LOW, LOW + slab), LOW + slab
    inside = {
        LOW - 1: jnp.where(first < 1, 0.0, 1.0),
        top: jnp.where(first + slab >= width, 0.0, 1.0),
        top + 1: jnp.where(first + slab + 1 >= width, 0.0, 1.0),
    }
    lax.fori_loop(0, window, products, 0)
    for w, keep in inside.items():
        apply(b_refs, 0, u1_refs, 1, w, (), (), keep)
    low_pairs, high_pairs = ((0, 0), (0, 1), (1, 1)), ((0, 1), (1, 1))
    lows = lax.fori_loop(
        *own,
        lambda w, c: apply(b_refs, 0, u1_refs, 1, w, c, low_pairs),
        (zero,) * 3 * len(parts),
        unroll=True,
    )
    apply(u1_refs, 1, u2_refs, LOW, top, (), (), inside[top])
    highs = lax.fori_loop(
        *own,
        lambda w, c: apply(u1_refs, 1, u2_refs, LOW, w, c, high_pairs),
        (zero,) * 2 * len(parts),
        unroll=True,
    )
    lasts = lax.fori_loop(*own, last, (zero,) * len(parts), unroll=True)
    column = lax.broadcasted_iota(jnp.int32, (128, 128), 1)
    trial = lax.broadcasted_iota(jnp.int32, (128, 128), 0) // width
    packed = [ref[...] for ref in packed_refs]
    for k, part in enumerate(parts):
        made = sh_ref[part * HALF : (part + 1) * HALF, :]
        moments = (*lows[3 * k : 3 * k + 3], *highs[2 * k : 2 * k + 2], lasts[k])
        for i, moment in enumerate(moments):
            made = made + dot(moment, jnp.where(column == 2 * i + trial, 1.0, 0.0))
        packed.append(made)
    if len(packed) * HALF == ORBS:
        for peer in range(group):
            for k, made in enumerate(packed):
                pay_ref[peer, k * HALF : (k + 1) * HALF, :] = made
    else:
        pay_ref[...] = packed[0]


def combine_kernel(
    slab, lines, width, group, share, flag_ref, pay_ref, v_ref, cy_ref, cz_ref, *refs
):
    o_refs, u_refs = refs[0:2], (refs[2:4], refs[4:6])
    out_ref, field_s = refs[6:]
    chunks = out_ref.shape[0]
    if share:
        rows = share * lines
        for k in range(chunks):
            out_ref[k, slab * lines : slab * lines + rows, :] = v_ref[
                k, pl.ds(flag_ref[2] * rows + LOW * lines, rows), :
            ]
    total = pay_ref[0]
    for k in range(1, group):
        total = total + pay_ref[k]
    row = lax.broadcasted_iota(jnp.int32, (128, 128), 0)
    half = lax.broadcasted_iota(jnp.int32, (128, 128), 1) // width
    m = [dot(total, jnp.where(row == 2 * k + half, 1.0, 0.0)) for k in range(MOMENTS)]
    shift = dot(total, jnp.where(row == SHIFT_LANE, 1.0, 0.0))
    inv = 1.0 / m[0]
    mu = [None] + [m[k] * inv * (8.0**-k) for k in range(1, MOMENTS)]
    sigma = 0.25 * (shift + CENTER)
    k00 = mu[1] + sigma
    k01 = mu[2] + sigma * mu[1]
    k11 = mu[3] + sigma * mu[2]
    k02 = k11
    k12 = mu[4] + sigma * mu[3]
    k22 = mu[5] + sigma * mu[4]
    r0 = 1.0 / k00
    l10 = k01 * r0
    l20 = k02 * r0
    d1 = k11 - l10 * k01
    t = k12 - l20 * k01
    l21 = t / d1
    d2 = k22 - l20 * k02 - l21 * t
    z1 = mu[1] - l10
    z2 = mu[2] - l20 - l21 * z1
    y2 = z2 / d2
    y1 = z1 / d1 - l21 * y2
    y0 = r0 - l10 * y1 - l20 * y2
    c0 = -0.25 * y0
    c1 = (-0.25 / 8.0) * y1
    c2 = (-0.25 / 64.0) * y2

    sublane = lax.broadcasted_iota(jnp.int32, (8, 128), 0)
    takes = [(sublane // step) % 2 == 0 for step in (1, 2, 4)]

    def merge(values):
        for take, step in zip(takes, (1, 2, 4)):
            values = [
                jnp.where(take, a, b) + pltpu.roll(jnp.where(take, b, a), step, 0)
                for a, b in zip(values[::2], values[1::2])
            ]
        return values[0]

    def plane(x, carry):
        w = x + LOW
        for y0 in range(0, width, 8):
            values = []
            for y in range(y0, y0 + 8):
                v = v_ref[y // lines, pl.ds(w * lines + y % lines, 1), :]
                both = []
                for k, (o_ref, (u1_ref, u2_ref)) in enumerate(zip(o_refs, u_refs)):
                    at = slice(k * HALF, (k + 1) * HALF)
                    o = o_ref[w, y]
                    u = c1[at] * u1_ref[x + LOW - 1, y] + c2[at] * u2_ref[x, y]
                    both.append(o * (c0[at] * (o * v) + u))
                values.append(both[0] + both[1])
            field_s[pl.ds(pl.multiple_of(x * width + y0, 8), 8), :] = merge(values)
        return carry

    lax.fori_loop(0, slab, plane, 0)
    turned = dot(field_s[...], cz_ref[...])
    turned = jnp.concatenate([turned[x * width : (x + 1) * width] for x in range(slab)], axis=1)
    planes = dot(cy_ref[...], turned)
    for x in range(slab):
        for k in range(chunks):
            out_ref[k, x * lines : (x + 1) * lines, :] = planes[
                k * lines : (k + 1) * lines, x * 128 : (x + 1) * 128
            ]


def gathered(got_ref, cx_ref, group):
    n = got_ref.shape[0]
    rows = cx_ref.shape[0] // group
    parts = []
    for j in range(group):
        parts.append(tree([got_ref[q * group + j, 0:rows, :] for q in range(n // group)]))
    return dot(cx_ref[...], jnp.concatenate(parts, axis=0))


def mapped_kernel(slab, lines, width, group, got_ref, cx_ref, mapped_ref, t_ref, pay_ref):
    n, size, _ = pay_ref.shape
    mapped = gathered(got_ref, cx_ref, group)
    mapped_ref[...] = mapped
    rounds = n // group
    rows = slab // rounds * lines
    for j in range(group):
        for q in range(rounds):
            at = (j * rounds + q) * rows
            t_ref[at : at + rows, :] = got_ref[q * group + j, slab * lines : slab * lines + rows, :]
    t = t_ref[...]
    sums = [jnp.sum(a * b, axis=0, keepdims=True) for a, b in ((t, t), (t, mapped), (mapped, mapped))]
    window = (slab + LOW + HIGH) * lines
    for k in range(n):
        start = (k % group) * slab * lines - LOW * lines
        low, high = max(start, 0), min(start + window, width * lines)
        pay_ref[k] = jnp.zeros((size, 128), F32)
        pay_ref[k, low - start : high - start, :] = mapped_ref[low:high, :]
        for i, s in enumerate(sums):
            pay_ref[k, window + i : window + i + 1, :] = s


def second_kernel(group, got_ref, cx_ref, t_ref, mapped_ref, cs_ref, second_ref):
    again = gathered(got_ref, cx_ref, group)
    center, inverse = cs_ref[0:1], cs_ref[1:2]
    t = t_ref[...]
    first = (mapped_ref[...] - center * t) * inverse
    second_ref[...] = 2.0 * (again - center * first) * inverse - t


def turn(x):
    return pltpu.roll(x, 64, x.ndim - 1)


def gram_kernel(per, second_ref, other_ref, pay_ref):
    n, size, _ = pay_ref.shape
    a, b = second_ref[...], other_ref[...]
    a1, b1 = turn(a), turn(b)
    pairs = ((a, a), (a, a1), (a, b), (a, b1), (b, b), (b, b1))
    sums = [jnp.sum(p * q, axis=0, keepdims=True) for p, q in pairs]
    block = jnp.concatenate(sums + [jnp.zeros((8 - len(sums), 128), F32)], axis=0)
    for k in range(n):
        pay_ref[k, 0:per, :] = second_ref[k * per : (k + 1) * per, :]
        pay_ref[k, size - 8 : size, :] = block


def final_kernel(per, width, flag_ref, got_ref, other_ref, out_ref, rows_s):
    n, size, _ = got_ref.shape
    total = tree([got_ref[k, size - 8 : size, :] for k in range(n)])
    total = dot(total, halves(8, width)) / float(width**3)
    swapped = turn(total)
    lane = lax.broadcasted_iota(jnp.int32, (1, 128), 1)
    in_first = lane < width
    is_low = jnp.zeros((1, 128), jnp.int32) + flag_ref[1] == 0

    def entry(k, t):
        here, there = total[k : k + 1], swapped[k : k + 1]
        return jnp.where(in_first, here, there) if t == 0 else jnp.where(in_first, there, here)

    aa = ((entry(0, 0), entry(1, 0)), (entry(1, 0), entry(0, 1)))
    bb = ((entry(4, 0), entry(5, 0)), (entry(5, 0), entry(4, 1)))
    ab = ((entry(2, 0), entry(3, 0)), (entry(3, 1), entry(2, 1)))
    m = [[None] * 4 for _ in range(4)]
    for i in range(2):
        for j in range(2):
            m[i][j] = jnp.where(is_low, aa[i][j], bb[i][j])
            m[2 + i][2 + j] = jnp.where(is_low, bb[i][j], aa[i][j])
            m[2 + j][i] = jnp.where(is_low, ab[i][j], ab[j][i])
    low = [[None] * 4 for _ in range(4)]
    inv = [[jnp.zeros((1, 128), F32)] * 4 for _ in range(4)]
    for j in range(4):
        pivot = m[j][j]
        for k in range(j):
            pivot = pivot - low[j][k] * low[j][k]
        inv[j][j] = 1.0 / jnp.sqrt(pivot)
        for i in range(j + 1, 4):
            value = m[i][j]
            for k in range(j):
                value = value - low[i][k] * low[j][k]
            low[i][j] = value * inv[j][j]
    for j in range(4):
        for i in range(j + 1, 4):
            value = low[i][j] * inv[j][j]
            for k in range(j + 1, i):
                value = value + low[i][k] * inv[k][j]
            inv[i][j] = -value * inv[i][i]

    def pick(i, j):
        return jnp.where(is_low, inv[i][j], inv[2 + i][(j + 2) % 4])

    c = [
        jnp.where(in_first, pick(0, a), pick(1, b)) for a, b in ((0, 1), (1, 0), (2, 3), (3, 2))
    ]
    for k in range(n):
        a, b = got_ref[k, 0:per, :], other_ref[k]
        rows_s[k] = (c[0] * a + c[1] * turn(a)) + (c[2] * b + c[3] * turn(b))
    planes = out_ref.shape[1]
    first_half = lax.broadcasted_iota(jnp.int32, (planes, 128), 1) < width
    lines = per // planes

    def line(y):
        return rows_s[y // lines, pl.ds(y % lines, planes, stride=lines), :]

    for pair in range(width // 2):
        even, odd = line(2 * pair), line(2 * pair + 1)
        at = slice(pair * 128, (pair + 1) * 128)
        out_ref[0, :, at] = jnp.where(first_half, even, turn(odd))
        out_ref[1, :, at] = jnp.where(first_half, turn(even), odd)


def vmem():
    return pl.BlockSpec(memory_space=pltpu.VMEM)


def smem():
    return pl.BlockSpec(memory_space=pltpu.SMEM)


def call(kernel, name, shapes, inputs, scratch=(), limit=4, in_smem=()):
    return pl.pallas_call(
        kernel,
        out_shape=shapes,
        in_specs=[smem() if k in in_smem else vmem() for k in range(len(inputs))],
        out_specs=jax.tree.map(lambda _: vmem(), shapes),
        scratch_shapes=scratch,
        compiler_params=pltpu.CompilerParams(vmem_limit_bytes=limit * MIB),
        name=name,
    )(*inputs)


def shape(*dims):
    return jax.ShapeDtypeStruct(dims, F32)


def up8(x):
    return -(-x // 8) * 8


def shards(n, cores, trials, orbitals, potential, coulomb, energies, frequencies, orbital_ids, freq_index):
    count, planes, cells = trials.shape
    held = orbitals.shape[0]
    width = coulomb.shape[1]
    lines = width // n
    group = ORBS // held
    slab = width // group
    window = slab + LOW + HIGH
    me = lax.axis_index("orb")
    core = lax.axis_index("trial")
    place = me % group
    pairs = cells // 128
    each = held // cores
    groups = [list(range(q * group, (q + 1) * group)) for q in range(n // group)]

    def swap(x):
        return lax.ppermute(x, "trial", [(k, (k + 1) % cores) for k in range(cores)])

    def exchange(x):
        return lax.all_to_all(x, "orb", split_axis=0, concat_axis=0, tiled=True)

    def exchange_group(x):
        return lax.all_to_all(
            x, "orb", split_axis=0, concat_axis=0, tiled=True, axis_index_groups=groups
        )

    mine = lax.dynamic_slice_in_dim(orbitals, core * each, each, 0).astype(F32)
    mine = mine.reshape(each, width * pairs, 128)
    sent = call(
        functools.partial(pack_kernel, slab, window, width, pairs),
        "pack_orbitals",
        shape(group, each * window * pairs, 128),
        (mine,),
        limit=8,
    )
    own_half = exchange_group(sent)
    own_half = own_half.reshape(HALF * window * pairs, 128)
    shifts = orbital_shifts(orbital_ids, freq_index, energies, frequencies)
    shifts = jnp.where(core == 0, shifts, jnp.roll(shifts, -each))
    slot_rows = [(k // each) * HALF + place * each + k % each for k in range(held)]
    row = lax.broadcasted_iota(jnp.int32, (ORBS, 128), 0)
    lane = lax.broadcasted_iota(jnp.int32, (ORBS, 128), 1)
    shift_rows = sum(
        jnp.where((row == slot_rows[k]) & (lane == SHIFT_LANE), shifts[k], 0.0) for k in range(held)
    )

    rounds = n // group
    flags = jnp.stack([place * slab, core, me // group]).astype(jnp.int32)
    fields = jnp.concatenate([trials, potential[None]], axis=0).reshape(count + 1, planes * pairs, 128)
    blocks = [
        lax.ppermute(
            fields,
            "orb",
            [
                (j * rounds + k, (k + r) % rounds * group + j)
                for j in range(group)
                for k in range(rounds)
            ],
        )
        for r in range(rounds)
    ]
    slabs = call(
        functools.partial(slab_kernel, rounds),
        "slab",
        shape(count + 1, slab * pairs, 128),
        (flags, *blocks),
        limit=8,
        in_smem=(0,),
    )
    if planes >= HIGH and rounds == 2:
        last = me % rounds == rounds - 1
        edge = jnp.where(last, fields[:, (planes - HIGH) * pairs :], fields[:, : HIGH * pairs])
        first, other = (
            lax.ppermute(
                edge,
                "orb",
                [((j - 1) * rounds + 1, q * group + j) for j in range(1, group)]
                + [((j + 1) * rounds, (1 - q) * group + j) for j in range(group - 1)],
            )
            for q in range(rounds)
        )
        is_first = me // group == 0
        low = jnp.where(is_first, first, other)[:, (HIGH - LOW) * pairs :]
        high = jnp.where(is_first, other, first)
    else:
        low = lax.ppermute(
            slabs[:, (slab - LOW) * pairs :], "orb", [(i, i + 1) for i in range(n) if i % group < group - 1]
        )
        high = lax.ppermute(slabs[:, : HIGH * pairs], "orb", [(i, i - 1) for i in range(n) if i % group > 0])
    used = window * lines
    trial_window, diag_window = call(
        functools.partial(fields_kernel, slab, lines, pairs),
        "fields",
        (shape(n, used, 128), shape(n, used, 128)),
        (slabs, low, high),
        limit=8,
    )
    cy = coulomb[1]
    cx, cz = call(
        functools.partial(factors_kernel, lines, width),
        "factors",
        (shape(width * lines, width * lines), shape(128, 128)),
        (coulomb,),
    )
    trial_window, diag_window, cx, cy, cz, shift_rows, own_half = lax.optimization_barrier(
        (trial_window, diag_window, cx, cy, cz, shift_rows, own_half)
    )
    spread_orbitals = [
        call(
            functools.partial(spread_kernel, window, pairs),
            "spread_orbitals",
            shape(window, width, HALF, 128),
            (rows,),
        )
        for rows in (own_half, swap(own_half))
    ]

    def krylov(parts, fields, packed):
        filtered = len(fields) == 2
        complete = len(packed) + len(parts) == 2
        shapes = [shape(slab + 3, width, HALF, 128), shape(slab + 1, width, HALF, 128)] * len(parts)
        shapes.append(shape(group, ORBS, 128) if complete else shape(HALF, 128))
        if filtered:
            shapes += [shape(n, used, 128), shape(8, 128)]
        return call(
            functools.partial(krylov_kernel, slab, lines, width, group, filtered, parts, len(packed)),
            "krylov",
            tuple(shapes),
            (flags, diag_window, shift_rows, *fields, *packed, *[spread_orbitals[k] for k in parts]),
            scratch=[pltpu.VMEM((len(parts), window, width, HALF, 128), F32)],
            limit=14,
            in_smem=(0,),
        )

    def combine(pay, v, us, share):
        part = call(
            functools.partial(combine_kernel, slab, lines, width, group, share),
            "combine",
            shape(n, up8((slab + share) * lines), 128),
            (flags, exchange_group(pay), v, cy, cz, *spread_orbitals, *us),
            scratch=[pltpu.VMEM((slab * width, 128), F32)],
            limit=4,
            in_smem=(0,),
        )
        return exchange(part)

    own_u1, own_u2, packed = krylov((0,), (trial_window,), ())
    other_u1, other_u2, pay = krylov((1,), (trial_window,), (packed,))
    got = combine(pay, trial_window, (own_u1, own_u2, other_u1, other_u2), slab // rounds)
    mapped, trial_rows, pay = call(
        functools.partial(mapped_kernel, slab, lines, width, group),
        "mapped",
        (shape(width * lines, 128), shape(width * lines, 128), shape(n, up8(used + 3), 128)),
        (got, cx),
    )
    made = krylov((0, 1), (trial_window, exchange(pay)), ())
    pay, v, scales = made[4:]
    got = combine(pay, v, made[:4], 0)
    second = call(
        functools.partial(second_kernel, group),
        "second",
        shape(width * lines, 128),
        (got, cx, trial_rows, mapped, scales),
    )
    per = planes * lines
    pay = call(functools.partial(gram_kernel, per), "gram", shape(n, up8(per) + 8, 128), (second, swap(second)))
    got = exchange(pay)
    return call(
        functools.partial(final_kernel, per, width),
        "final",
        shape(count, planes, cells),
        (flags, got, swap(got[:, :per])),
        scratch=[pltpu.VMEM((n, per, 128), F32)],
        in_smem=(0,),
    )


def solution(mesh):
    n, cores = mesh.shape["orb"], mesh.shape["trial"]
    in_specs = (
        P("trial", "orb", None), P("orb", None, None), P("orb", None), P(), P(), P(), P("orb"), P("orb"),
    )
    return jax.shard_map(
        functools.partial(shards, n, cores),
        mesh=mesh, in_specs=in_specs, out_specs=P("trial", "orb", None), check_vma=False,
    )
```

```python
import functools
import jax
import jax.numpy as jnp
from jax import lax
from jax.experimental import pallas as pl
from jax.experimental.pallas import tpu as pltpu
from jax.sharding import PartitionSpec as P

LOW = 2
HIGH = 3
CENTER = 4.25
ORBS = 16
HALF = 8
SHIFT_LANE = 12
MOMENTS = 6
HIGHEST = lax.Precision.HIGHEST
F32 = jnp.float32
MIB = 2**20


def dot(a, b):
    return jnp.dot(a, b, precision=HIGHEST, preferred_element_type=F32)


def halves(rows, width, value=1.0):
    a = lax.broadcasted_iota(jnp.int32, (128, 128), 0) // width
    b = lax.broadcasted_iota(jnp.int32, (128, 128), 1) // width
    return jnp.where(a == b, 1.0, 0.0)


def tree(terms):
    while len(terms) > 1:
        odd = [terms[-1]] if len(terms) % 2 else []
        terms = [a + b for a, b in zip(terms[::2], terms[1::2])] + odd
    return terms[0]


def orbital_shifts(orbital_ids, freq_index, energies, frequencies):
    energy_slots = lax.broadcasted_iota(jnp.int32, (1, energies.shape[0]), 1)
    picked_energy = jnp.sum(
        jnp.where(orbital_ids[:, None] == energy_slots, energies[None, :], 0.0), axis=1
    )
    freq_slots = lax.broadcasted_iota(jnp.int32, (1, frequencies.shape[0]), 1)
    picked_freq = jnp.sum(
        jnp.where(freq_index[:, None] == freq_slots, frequencies[None, :], 0.0), axis=1
    )
    return picked_freq - picked_energy


def spread_kernel(window, pairs, src_ref, dst_ref, rows_s):
    rows = window * pairs
    stride = rows + 1
    first_half = lax.broadcasted_iota(jnp.int32, (HALF, 128), 1) < 64
    for k in range(HALF):
        rows_s[k * stride : k * stride + rows, :] = src_ref[k * rows : (k + 1) * rows, :]
    for w in range(window):
        for i in range(pairs):
            pair = rows_s[pl.ds(w * pairs + i, HALF, stride=stride), :]
            turned = pltpu.roll(pair, 64, 1)
            dst_ref[w, 2 * i] = jnp.where(first_half, pair, turned)
            dst_ref[w, 2 * i + 1] = jnp.where(first_half, turned, pair)


def pack_kernel(slab, window, width, pairs, src_ref, dst_ref):
    each = src_ref.shape[0]
    size = window * pairs
    for j in range(dst_ref.shape[0]):
        start = (j * slab - LOW) * pairs
        low, high = max(start, 0), min(start + size, width * pairs)
        for e in range(each):
            if low > start:
                dst_ref[j, e * size : e * size + low - start, :] = jnp.zeros((low - start, 128), F32)
            if high < start + size:
                dst_ref[j, e * size + high - start : (e + 1) * size, :] = jnp.zeros(
                    (start + size - high, 128), F32
                )
            dst_ref[j, e * size + low - start : e * size + high - start, :] = src_ref[e, low:high, :]


def equal(rows, columns, left, right):
    a = lax.broadcasted_iota(jnp.int32, (rows, columns), 0)
    b = lax.broadcasted_iota(jnp.int32, (rows, columns), 1)
    return left(a) == right(b)


def factors_kernel(lines, width, c_ref, cx_ref, cz_ref):
    size = width * lines
    pick = jnp.where(equal(size, width, lambda a: a // lines, lambda b: b), 1.0, 0.0)
    turned = jnp.where(equal(width, size, lambda a: a, lambda b: b // lines), 1.0, 0.0)
    same = equal(size, size, lambda a: a % lines, lambda b: b % lines)
    cx_ref[...] = jnp.where(same, dot(dot(pick, c_ref[0]), turned), 0.0)
    pick = jnp.where(equal(128, width, lambda a: a % width, lambda b: b), 1.0, 0.0)
    turned = jnp.where(equal(width, 128, lambda a: a, lambda b: b % width), 1.0, 0.0)
    same = equal(128, 128, lambda a: a // width, lambda b: b // width)
    cz_ref[...] = jnp.where(same, dot(dot(pick, c_ref[2].T), turned), 0.0)


def slab_kernel(rounds, flag_ref, *refs):
    dst_ref = refs[rounds]
    rows = refs[0].shape[1]
    for r in range(rounds):
        k = lax.rem(flag_ref[2] - r + rounds, rounds)
        dst_ref[:, pl.ds(pl.multiple_of(k * rows, 8), rows), :] = refs[r][...]


def fields_kernel(slab, lines, pairs, slab_ref, low_ref, high_ref, v_ref, d_ref):
    first_half = lax.broadcasted_iota(jnp.int32, (8, 128), 1) < 64

    def both(a, b):
        return jnp.where(first_half, a, turn(b)), jnp.where(first_half, turn(a), b)

    for w in range(slab + LOW + HIGH):
        if w < LOW:
            ref, at = low_ref, w
        elif w < LOW + slab:
            ref, at = slab_ref, w - LOW
        else:
            ref, at = high_ref, w - LOW - slab
        for rb in range(pairs // 8):
            rows = slice(at * pairs + 8 * rb, at * pairs + 8 * rb + 8)
            v = both(ref[0, rows, :], ref[1, rows, :])
            diag = 2.0 * (3.0 - CENTER + ref[2, rows, :])
            d = both(diag, diag)
            for i in range(8):
                for h in range(2):
                    y = 2 * (8 * rb + i) + h
                    row = w * lines + y % lines
                    v_ref[y // lines, row : row + 1, :] = v[h][i : i + 1]
                    d_ref[y // lines, row : row + 1, :] = d[h][i : i + 1]


def krylov_kernel(slab, lines, width, group, filtered, parts, before, *refs):
    refs = list(refs)
    take = lambda k: [refs.pop(0) for _ in range(k)]
    flag_ref, d_ref, sh_ref, t_ref = take(4)
    (m_ref,) = take(1) if filtered else (None,)
    packed_refs = take(before)
    o_refs = take(len(parts))
    u_refs = [take(2) for _ in parts]
    (pay_ref,) = take(1)
    v_ref, cs_ref = take(2) if filtered else (t_ref, None)
    (b_s,) = refs
    window = slab + LOW + HIGH
    lane = lax.broadcasted_iota(jnp.int32, (HALF, 128), 1)
    at_low = lane % width == 0
    at_high = lane % width == width - 1
    zero = jnp.zeros((HALF, 128), F32)
    n = t_ref.shape[0]

    if filtered:
        base = window * lines
        total = m_ref[0, base : base + 3, :]
        for k in range(1, n):
            total = total + m_ref[k, base : base + 3, :]
        total = jnp.concatenate([total, jnp.zeros((5, 128), F32)], axis=0)
        total = dot(total, halves(8, width))
        center = total[1:2] / total[0:1]
        inverse = 1.0 / jnp.sqrt(total[2:3] / total[0:1])
        cs_ref[0:1] = center
        cs_ref[1:2] = inverse
        used = v_ref.shape[1]
        for k in range(n):
            v_ref[k] = (m_ref[k, 0:used, :] - center * t_ref[k, 0:used, :]) * inverse

    def v_row(w, y):
        return v_ref[y // lines, pl.ds(w * lines + y % lines, 1), :]

    def d_row(w, y):
        return d_ref[y // lines, pl.ds(w * lines + y % lines, 1), :]

    b_refs = [b_s.at[k] for k in range(len(parts))]
    u1_refs, u2_refs = zip(*u_refs)

    def products(w, carry):
        for y in range(width):
            v = v_row(w, y)
            for b_ref, o_ref in zip(b_refs, o_refs):
                b_ref[w, y] = o_ref[w, y] * v
        return carry

    def apply(srcs, src_at, dsts, dst_at, w, carry, pairs, keep=None):
        fields = [[zero] + [src[w - src_at, y] for y in range(width)] + [zero] for src in srcs]
        terms = [[] for _ in srcs for _ in pairs]
        for y in range(width):
            diag = d_row(w, y)
            for k, (rows, src, dst) in enumerate(zip(fields, srcs, dsts)):
                mid = rows[y + 1]
                around = (rows[y] + rows[y + 2]) + (src[w - 1 - src_at, y] + src[w + 1 - src_at, y])
                around = around + (
                    jnp.where(at_low, 0.0, pltpu.roll(mid, 1, 1))
                    + jnp.where(at_high, 0.0, pltpu.roll(mid, 127, 1))
                )
                new = diag * mid - around
                if keep is not None:
                    new = new * keep
                dst[w - dst_at, y] = new
                both = (mid, new)
                for i, (a, b) in enumerate(pairs):
                    terms[k * len(pairs) + i].append(both[a] * both[b])
        return tuple(old + tree(t) for old, t in zip(carry, terms))

    def last(w, carry):
        fields = [[u2_ref[w - LOW, y] for y in range(width)] + [zero] for u2_ref in u2_refs]
        terms = [[] for _ in fields]
        for y in range(width):
            diag = d_row(w, y)
            for k, (rows, u2_ref) in enumerate(zip(fields, u2_refs)):
                mid = rows[y]
                above = (rows[y + 1] + u2_ref[w + 1 - LOW, y]) + jnp.where(
                    at_high, 0.0, pltpu.roll(mid, 127, 1)
                )
                terms[k].append(mid * (diag * mid - 2.0 * above))
        return tuple(old + tree(t) for old, t in zip(carry, terms))

    first = flag_ref[0]
    own, top = (LOW, LOW + slab), LOW + slab
    inside = {
        LOW - 1: jnp.where(first < 1, 0.0, 1.0),
        top: jnp.where(first + slab >= width, 0.0, 1.0),
        top + 1: jnp.where(first + slab + 1 >= width, 0.0, 1.0),
    }
    lax.fori_loop(0, window, products, 0, unroll=True)
    for w, keep in inside.items():
        apply(b_refs, 0, u1_refs, 1, w, (), (), keep)
    low_pairs, high_pairs = ((0, 0), (0, 1), (1, 1)), ((0, 1), (1, 1))
    lows = lax.fori_loop(
        *own,
        lambda w, c: apply(b_refs, 0, u1_refs, 1, w, c, low_pairs),
        (zero,) * 3 * len(parts),
        unroll=True,
    )
    apply(u1_refs, 1, u2_refs, LOW, top, (), (), inside[top])
    highs = lax.fori_loop(
        *own,
        lambda w, c: apply(u1_refs, 1, u2_refs, LOW, w, c, high_pairs),
        (zero,) * 2 * len(parts),
        unroll=True,
    )
    lasts = lax.fori_loop(*own, last, (zero,) * len(parts), unroll=True)
    column = lax.broadcasted_iota(jnp.int32, (128, 128), 1)
    trial = lax.broadcasted_iota(jnp.int32, (128, 128), 0) // width
    packed = [ref[...] for ref in packed_refs]
    for k, part in enumerate(parts):
        made = sh_ref[part * HALF : (part + 1) * HALF, :]
        moments = (*lows[3 * k : 3 * k + 3], *highs[2 * k : 2 * k + 2], lasts[k])
        for i, moment in enumerate(moments):
            made = made + dot(moment, jnp.where(column == 2 * i + trial, 1.0, 0.0))
        packed.append(made)
    if len(packed) * HALF == ORBS:
        for peer in range(group):
            for k, made in enumerate(packed):
                pay_ref[peer, k * HALF : (k + 1) * HALF, :] = made
    else:
        pay_ref[...] = packed[0]


def combine_kernel(
    slab, lines, width, group, share, flag_ref, pay_ref, v_ref, cy_ref, cz_ref, *refs
):
    o_refs, u_refs = refs[0:2], (refs[2:4], refs[4:6])
    out_ref, field_s = refs[6:]
    chunks = out_ref.shape[0]
    if share:
        rows = share * lines
        for k in range(chunks):
            out_ref[k, slab * lines : slab * lines + rows, :] = v_ref[
                k, pl.ds(flag_ref[2] * rows + LOW * lines, rows), :
            ]
    total = pay_ref[0]
    for k in range(1, group):
        total = total + pay_ref[k]
    row = lax.broadcasted_iota(jnp.int32, (128, 128), 0)
    half = lax.broadcasted_iota(jnp.int32, (128, 128), 1) // width
    m = [dot(total, jnp.where(row == 2 * k + half, 1.0, 0.0)) for k in range(MOMENTS)]
    shift = dot(total, jnp.where(row == SHIFT_LANE, 1.0, 0.0))
    inv = 1.0 / m[0]
    mu = [None] + [m[k] * inv * (8.0**-k) for k in range(1, MOMENTS)]
    sigma = 0.25 * (shift + CENTER)
    k00 = mu[1] + sigma
    k01 = mu[2] + sigma * mu[1]
    k11 = mu[3] + sigma * mu[2]
    k02 = k11
    k12 = mu[4] + sigma * mu[3]
    k22 = mu[5] + sigma * mu[4]
    r0 = 1.0 / k00
    l10 = k01 * r0
    l20 = k02 * r0
    d1 = k11 - l10 * k01
    t = k12 - l20 * k01
    l21 = t / d1
    d2 = k22 - l20 * k02 - l21 * t
    z1 = mu[1] - l10
    z2 = mu[2] - l20 - l21 * z1
    y2 = z2 / d2
    y1 = z1 / d1 - l21 * y2
    y0 = r0 - l10 * y1 - l20 * y2
    c0 = -0.25 * y0
    c1 = (-0.25 / 8.0) * y1
    c2 = (-0.25 / 64.0) * y2

    sublane = lax.broadcasted_iota(jnp.int32, (8, 128), 0)
    takes = [(sublane // step) % 2 == 0 for step in (1, 2, 4)]

    def merge(values):
        for take, step in zip(takes, (1, 2, 4)):
            values = [
                jnp.where(take, a, b) + pltpu.roll(jnp.where(take, b, a), step, 0)
                for a, b in zip(values[::2], values[1::2])
            ]
        return values[0]

    def plane(x, carry):
        w = x + LOW
        for y0 in range(0, width, 8):
            values = []
            for y in range(y0, y0 + 8):
                v = v_ref[y // lines, pl.ds(w * lines + y % lines, 1), :]
                both = []
                for k, (o_ref, (u1_ref, u2_ref)) in enumerate(zip(o_refs, u_refs)):
                    at = slice(k * HALF, (k + 1) * HALF)
                    o = o_ref[w, y]
                    u = c1[at] * u1_ref[x + LOW - 1, y] + c2[at] * u2_ref[x, y]
                    both.append(o * (c0[at] * (o * v) + u))
                values.append(both[0] + both[1])
            field_s[pl.ds(pl.multiple_of(x * width + y0, 8), 8), :] = merge(values)
        return carry

    lax.fori_loop(0, slab, plane, 0)
    turned = dot(field_s[...], cz_ref[...])
    turned = jnp.concatenate([turned[x * width : (x + 1) * width] for x in range(slab)], axis=1)
    planes = dot(cy_ref[...], turned)
    for x in range(slab):
        for k in range(chunks):
            out_ref[k, x * lines : (x + 1) * lines, :] = planes[
                k * lines : (k + 1) * lines, x * 128 : (x + 1) * 128
            ]


def gathered(got_ref, cx_ref, group):
    n = got_ref.shape[0]
    rows = cx_ref.shape[0] // group
    parts = []
    for j in range(group):
        parts.append(tree([got_ref[q * group + j, 0:rows, :] for q in range(n // group)]))
    return dot(cx_ref[...], jnp.concatenate(parts, axis=0))


def mapped_kernel(slab, lines, width, group, got_ref, cx_ref, mapped_ref, t_ref, pay_ref):
    n, size, _ = pay_ref.shape
    mapped = gathered(got_ref, cx_ref, group)
    mapped_ref[...] = mapped
    rounds = n // group
    rows = slab // rounds * lines
    for j in range(group):
        for q in range(rounds):
            at = (j * rounds + q) * rows
            t_ref[at : at + rows, :] = got_ref[q * group + j, slab * lines : slab * lines + rows, :]
    t = t_ref[...]
    sums = [jnp.sum(a * b, axis=0, keepdims=True) for a, b in ((t, t), (t, mapped), (mapped, mapped))]
    window = (slab + LOW + HIGH) * lines
    for k in range(n):
        start = (k % group) * slab * lines - LOW * lines
        low, high = max(start, 0), min(start + window, width * lines)
        pay_ref[k] = jnp.zeros((size, 128), F32)
        pay_ref[k, low - start : high - start, :] = mapped_ref[low:high, :]
        for i, s in enumerate(sums):
            pay_ref[k, window + i : window + i + 1, :] = s


def second_kernel(group, got_ref, cx_ref, t_ref, mapped_ref, cs_ref, second_ref):
    again = gathered(got_ref, cx_ref, group)
    center, inverse = cs_ref[0:1], cs_ref[1:2]
    t = t_ref[...]
    first = (mapped_ref[...] - center * t) * inverse
    second_ref[...] = 2.0 * (again - center * first) * inverse - t


def turn(x):
    return pltpu.roll(x, 64, x.ndim - 1)


def gram_kernel(per, second_ref, other_ref, pay_ref):
    n, size, _ = pay_ref.shape
    a, b = second_ref[...], other_ref[...]
    a1, b1 = turn(a), turn(b)
    pairs = ((a, a), (a, a1), (a, b), (a, b1), (b, b), (b, b1))
    sums = [jnp.sum(p * q, axis=0, keepdims=True) for p, q in pairs]
    block = jnp.concatenate(sums + [jnp.zeros((8 - len(sums), 128), F32)], axis=0)
    for k in range(n):
        pay_ref[k, 0:per, :] = second_ref[k * per : (k + 1) * per, :]
        pay_ref[k, size - 8 : size, :] = block


def final_kernel(per, width, flag_ref, got_ref, other_ref, out_ref, rows_s):
    n, size, _ = got_ref.shape
    total = tree([got_ref[k, size - 8 : size, :] for k in range(n)])
    total = dot(total, halves(8, width)) / float(width**3)
    swapped = turn(total)
    lane = lax.broadcasted_iota(jnp.int32, (1, 128), 1)
    in_first = lane < width
    is_low = jnp.zeros((1, 128), jnp.int32) + flag_ref[1] == 0

    def entry(k, t):
        here, there = total[k : k + 1], swapped[k : k + 1]
        return jnp.where(in_first, here, there) if t == 0 else jnp.where(in_first, there, here)

    aa = ((entry(0, 0), entry(1, 0)), (entry(1, 0), entry(0, 1)))
    bb = ((entry(4, 0), entry(5, 0)), (entry(5, 0), entry(4, 1)))
    ab = ((entry(2, 0), entry(3, 0)), (entry(3, 1), entry(2, 1)))
    m = [[None] * 4 for _ in range(4)]
    for i in range(2):
        for j in range(2):
            m[i][j] = jnp.where(is_low, aa[i][j], bb[i][j])
            m[2 + i][2 + j] = jnp.where(is_low, bb[i][j], aa[i][j])
            m[2 + j][i] = jnp.where(is_low, ab[i][j], ab[j][i])
    low = [[None] * 4 for _ in range(4)]
    inv = [[jnp.zeros((1, 128), F32)] * 4 for _ in range(4)]
    for j in range(4):
        pivot = m[j][j]
        for k in range(j):
            pivot = pivot - low[j][k] * low[j][k]
        inv[j][j] = 1.0 / jnp.sqrt(pivot)
        for i in range(j + 1, 4):
            value = m[i][j]
            for k in range(j):
                value = value - low[i][k] * low[j][k]
            low[i][j] = value * inv[j][j]
    for j in range(4):
        for i in range(j + 1, 4):
            value = low[i][j] * inv[j][j]
            for k in range(j + 1, i):
                value = value + low[i][k] * inv[k][j]
            inv[i][j] = -value * inv[i][i]

    def pick(i, j):
        return jnp.where(is_low, inv[i][j], inv[2 + i][(j + 2) % 4])

    c = [
        jnp.where(in_first, pick(0, a), pick(1, b)) for a, b in ((0, 1), (1, 0), (2, 3), (3, 2))
    ]
    for k in range(n):
        a, b = got_ref[k, 0:per, :], other_ref[k]
        rows_s[k] = (c[0] * a + c[1] * turn(a)) + (c[2] * b + c[3] * turn(b))
    planes = out_ref.shape[1]
    first_half = lax.broadcasted_iota(jnp.int32, (planes, 128), 1) < width
    lines = per // planes

    def line(y):
        return rows_s[y // lines, pl.ds(y % lines, planes, stride=lines), :]

    for pair in range(width // 2):
        even, odd = line(2 * pair), line(2 * pair + 1)
        at = slice(pair * 128, (pair + 1) * 128)
        out_ref[0, :, at] = jnp.where(first_half, even, turn(odd))
        out_ref[1, :, at] = jnp.where(first_half, turn(even), odd)


def vmem():
    return pl.BlockSpec(memory_space=pltpu.VMEM)


def smem():
    return pl.BlockSpec(memory_space=pltpu.SMEM)


def call(kernel, name, shapes, inputs, scratch=(), limit=4, in_smem=()):
    return pl.pallas_call(
        kernel,
        out_shape=shapes,
        in_specs=[smem() if k in in_smem else vmem() for k in range(len(inputs))],
        out_specs=jax.tree.map(lambda _: vmem(), shapes),
        scratch_shapes=scratch,
        compiler_params=pltpu.CompilerParams(vmem_limit_bytes=limit * MIB),
        name=name,
    )(*inputs)


def shape(*dims):
    return jax.ShapeDtypeStruct(dims, F32)


def up8(x):
    return -(-x // 8) * 8


def shards(n, cores, trials, orbitals, potential, coulomb, energies, frequencies, orbital_ids, freq_index):
    count, planes, cells = trials.shape
    held = orbitals.shape[0]
    width = coulomb.shape[1]
    lines = width // n
    group = ORBS // held
    slab = width // group
    window = slab + LOW + HIGH
    me = lax.axis_index("orb")
    core = lax.axis_index("trial")
    place = me % group
    pairs = cells // 128
    each = held // cores
    groups = [list(range(q * group, (q + 1) * group)) for q in range(n // group)]

    def swap(x):
        return lax.ppermute(x, "trial", [(k, (k + 1) % cores) for k in range(cores)])

    def exchange(x):
        return lax.all_to_all(x, "orb", split_axis=0, concat_axis=0, tiled=True)

    def exchange_group(x):
        return lax.all_to_all(
            x, "orb", split_axis=0, concat_axis=0, tiled=True, axis_index_groups=groups
        )

    mine = lax.dynamic_slice_in_dim(orbitals, core * each, each, 0).astype(F32)
    mine = mine.reshape(each, width * pairs, 128)
    sent = call(
        functools.partial(pack_kernel, slab, window, width, pairs),
        "pack_orbitals",
        shape(group, each * window * pairs, 128),
        (mine,),
        limit=8,
    )
    own_half = exchange_group(sent)
    own_half = own_half.reshape(HALF * window * pairs, 128)
    shifts = orbital_shifts(orbital_ids, freq_index, energies, frequencies)
    shifts = jnp.where(core == 0, shifts, jnp.roll(shifts, -each))
    slot_rows = [(k // each) * HALF + place * each + k % each for k in range(held)]
    row = lax.broadcasted_iota(jnp.int32, (ORBS, 128), 0)
    lane = lax.broadcasted_iota(jnp.int32, (ORBS, 128), 1)
    shift_rows = sum(
        jnp.where((row == slot_rows[k]) & (lane == SHIFT_LANE), shifts[k], 0.0) for k in range(held)
    )

    rounds = n // group
    flags = jnp.stack([place * slab, core, me // group]).astype(jnp.int32)
    fields = jnp.concatenate([trials, potential[None]], axis=0).reshape(count + 1, planes * pairs, 128)
    blocks = [
        lax.ppermute(
            fields,
            "orb",
            [
                (j * rounds + k, (k + r) % rounds * group + j)
                for j in range(group)
                for k in range(rounds)
            ],
        )
        for r in range(rounds)
    ]
    slabs = call(
        functools.partial(slab_kernel, rounds),
        "slab",
        shape(count + 1, slab * pairs, 128),
        (flags, *blocks),
        limit=8,
        in_smem=(0,),
    )
    if planes >= HIGH and rounds == 2:
        last = me % rounds == rounds - 1
        edge = jnp.where(last, fields[:, (planes - HIGH) * pairs :], fields[:, : HIGH * pairs])
        first, other = (
            lax.ppermute(
                edge,
                "orb",
                [((j - 1) * rounds + 1, q * group + j) for j in range(1, group)]
                + [((j + 1) * rounds, (1 - q) * group + j) for j in range(group - 1)],
            )
            for q in range(rounds)
        )
        is_first = me // group == 0
        low = jnp.where(is_first, first, other)[:, (HIGH - LOW) * pairs :]
        high = jnp.where(is_first, other, first)
    else:
        low = lax.ppermute(
            slabs[:, (slab - LOW) * pairs :], "orb", [(i, i + 1) for i in range(n) if i % group < group - 1]
        )
        high = lax.ppermute(slabs[:, : HIGH * pairs], "orb", [(i, i - 1) for i in range(n) if i % group > 0])
    used = window * lines
    trial_window, diag_window = call(
        functools.partial(fields_kernel, slab, lines, pairs),
        "fields",
        (shape(n, used, 128), shape(n, used, 128)),
        (slabs, low, high),
        limit=8,
    )
    cy = coulomb[1]
    cx, cz = call(
        functools.partial(factors_kernel, lines, width),
        "factors",
        (shape(width * lines, width * lines), shape(128, 128)),
        (coulomb,),
    )
    trial_window, diag_window, cx, cy, cz, shift_rows, own_half = lax.optimization_barrier(
        (trial_window, diag_window, cx, cy, cz, shift_rows, own_half)
    )
    spread_orbitals = [
        call(
            functools.partial(spread_kernel, window, pairs),
            "spread_orbitals",
            shape(window, width, HALF, 128),
            (rows,),
            scratch=[pltpu.VMEM((HALF * (window * pairs + 1), 128), F32)],
        )
        for rows in (own_half, swap(own_half))
    ]

    def krylov(parts, fields, packed):
        filtered = len(fields) == 2
        complete = len(packed) + len(parts) == 2
        shapes = [shape(slab + 3, width, HALF, 128), shape(slab + 1, width, HALF, 128)] * len(parts)
        shapes.append(shape(group, ORBS, 128) if complete else shape(HALF, 128))
        if filtered:
            shapes += [shape(n, used, 128), shape(8, 128)]
        return call(
            functools.partial(krylov_kernel, slab, lines, width, group, filtered, parts, len(packed)),
            "krylov",
            tuple(shapes),
            (flags, diag_window, shift_rows, *fields, *packed, *[spread_orbitals[k] for k in parts]),
            scratch=[pltpu.VMEM((len(parts), window, width, HALF, 128), F32)],
            limit=14,
            in_smem=(0,),
        )

    def combine(pay, v, us, share):
        part = call(
            functools.partial(combine_kernel, slab, lines, width, group, share),
            "combine",
            shape(n, up8((slab + share) * lines), 128),
            (flags, exchange_group(pay), v, cy, cz, *spread_orbitals, *us),
            scratch=[pltpu.VMEM((slab * width, 128), F32)],
            limit=4,
            in_smem=(0,),
        )
        return exchange(part)

    own_u1, own_u2, packed = krylov((0,), (trial_window,), ())
    other_u1, other_u2, pay = krylov((1,), (trial_window,), (packed,))
    got = combine(pay, trial_window, (own_u1, own_u2, other_u1, other_u2), slab // rounds)
    mapped, trial_rows, pay = call(
        functools.partial(mapped_kernel, slab, lines, width, group),
        "mapped",
        (shape(width * lines, 128), shape(width * lines, 128), shape(n, up8(used + 3), 128)),
        (got, cx),
    )
    made = krylov((0, 1), (trial_window, exchange(pay)), ())
    pay, v, scales = made[4:]
    got = combine(pay, v, made[:4], 0)
    second = call(
        functools.partial(second_kernel, group),
        "second",
        shape(width * lines, 128),
        (got, cx, trial_rows, mapped, scales),
    )
    per = planes * lines
    pay = call(functools.partial(gram_kernel, per), "gram", shape(n, up8(per) + 8, 128), (second, swap(second)))
    got = exchange(pay)
    return call(
        functools.partial(final_kernel, per, width),
        "final",
        shape(count, planes, cells),
        (flags, got, swap(got[:, :per])),
        scratch=[pltpu.VMEM((n, per, 128), F32)],
        in_smem=(0,),
    )


def solution(mesh):
    n, cores = mesh.shape["orb"], mesh.shape["trial"]
    in_specs = (
        P("trial", "orb", None), P("orb", None, None), P("orb", None), P(), P(), P(), P("orb"), P("orb"),
    )
    return jax.shard_map(
        functools.partial(shards, n, cores),
        mesh=mesh, in_specs=in_specs, out_specs=P("trial", "orb", None), check_vma=False,
    )
```

```python
import functools
import jax
import jax.numpy as jnp
from jax import lax
from jax.experimental import pallas as pl
from jax.experimental.pallas import tpu as pltpu
from jax.sharding import PartitionSpec as P

LOW = 2
HIGH = 3
CENTER = 4.25
ORBS = 16
HALF = 8
SHIFT_LANE = 12
MOMENTS = 6
HIGHEST = lax.Precision.HIGHEST
F32 = jnp.float32
MIB = 2**20


def dot(a, b):
    return jnp.dot(a, b, precision=HIGHEST, preferred_element_type=F32)


def halves(rows, width, value=1.0):
    a = lax.broadcasted_iota(jnp.int32, (128, 128), 0) // width
    b = lax.broadcasted_iota(jnp.int32, (128, 128), 1) // width
    return jnp.where(a == b, 1.0, 0.0)


def tree(terms):
    while len(terms) > 1:
        odd = [terms[-1]] if len(terms) % 2 else []
        terms = [a + b for a, b in zip(terms[::2], terms[1::2])] + odd
    return terms[0]


def orbital_shifts(orbital_ids, freq_index, energies, frequencies):
    energy_slots = lax.broadcasted_iota(jnp.int32, (1, energies.shape[0]), 1)
    picked_energy = jnp.sum(
        jnp.where(orbital_ids[:, None] == energy_slots, energies[None, :], 0.0), axis=1
    )
    freq_slots = lax.broadcasted_iota(jnp.int32, (1, frequencies.shape[0]), 1)
    picked_freq = jnp.sum(
        jnp.where(freq_index[:, None] == freq_slots, frequencies[None, :], 0.0), axis=1
    )
    return picked_freq - picked_energy


def placed(k, crossed):
    return k // 4 * 4 + k % 2 * 2 + k // 2 % 2 if crossed else k


def spread_kernel(window, pairs, src_ref, dst_ref, rows_s):
    rows = window * pairs
    stride = rows + 1
    first_half = lax.broadcasted_iota(jnp.int32, (HALF, 128), 1) < 64
    for k in range(HALF):
        rows_s[k * stride : k * stride + rows, :] = src_ref[k * rows : (k + 1) * rows, :]
    for w in range(window):
        for i in range(pairs):
            pair = rows_s[pl.ds(w * pairs + i, HALF, stride=stride), :]
            turned = pltpu.roll(pair, 64, 1)
            dst_ref[w, 2 * i] = jnp.where(first_half, pair, turned)
            dst_ref[w, 2 * i + 1] = jnp.where(first_half, turned, pair)


def pack_kernel(slab, window, width, pairs, crossed, src_ref, dst_ref):
    each = src_ref.shape[0]
    size = window * pairs
    for j in range(dst_ref.shape[0]):
        start = (placed(j, crossed) * slab - LOW) * pairs
        low, high = max(start, 0), min(start + size, width * pairs)
        for e in range(each):
            if low > start:
                dst_ref[j, e * size : e * size + low - start, :] = jnp.zeros((low - start, 128), F32)
            if high < start + size:
                dst_ref[j, e * size + high - start : (e + 1) * size, :] = jnp.zeros(
                    (start + size - high, 128), F32
                )
            dst_ref[j, e * size + low - start : e * size + high - start, :] = src_ref[e, low:high, :]


def equal(rows, columns, left, right):
    a = lax.broadcasted_iota(jnp.int32, (rows, columns), 0)
    b = lax.broadcasted_iota(jnp.int32, (rows, columns), 1)
    return left(a) == right(b)


def factors_kernel(lines, width, c_ref, cx_ref, cz_ref):
    size = width * lines
    pick = jnp.where(equal(size, width, lambda a: a // lines, lambda b: b), 1.0, 0.0)
    turned = jnp.where(equal(width, size, lambda a: a, lambda b: b // lines), 1.0, 0.0)
    same = equal(size, size, lambda a: a % lines, lambda b: b % lines)
    cx_ref[...] = jnp.where(same, dot(dot(pick, c_ref[0]), turned), 0.0)
    pick = jnp.where(equal(128, width, lambda a: a % width, lambda b: b), 1.0, 0.0)
    turned = jnp.where(equal(width, 128, lambda a: a, lambda b: b % width), 1.0, 0.0)
    same = equal(128, 128, lambda a: a // width, lambda b: b // width)
    cz_ref[...] = jnp.where(same, dot(dot(pick, c_ref[2].T), turned), 0.0)


def slab_kernel(rounds, flag_ref, *refs):
    dst_ref = refs[rounds]
    rows = refs[0].shape[1]
    for r in range(rounds):
        k = lax.rem(flag_ref[2] - r + rounds, rounds)
        dst_ref[:, pl.ds(pl.multiple_of(k * rows, 8), rows), :] = refs[r][...]


def fields_kernel(slab, lines, pairs, slab_ref, low_ref, high_ref, v_ref, d_ref):
    first_half = lax.broadcasted_iota(jnp.int32, (8, 128), 1) < 64

    def both(a, b):
        return jnp.where(first_half, a, turn(b)), jnp.where(first_half, turn(a), b)

    for w in range(slab + LOW + HIGH):
        if w < LOW:
            ref, at = low_ref, w
        elif w < LOW + slab:
            ref, at = slab_ref, w - LOW
        else:
            ref, at = high_ref, w - LOW - slab
        for rb in range(pairs // 8):
            rows = slice(at * pairs + 8 * rb, at * pairs + 8 * rb + 8)
            v = both(ref[0, rows, :], ref[1, rows, :])
            diag = 2.0 * (3.0 - CENTER + ref[2, rows, :])
            d = both(diag, diag)
            for i in range(8):
                for h in range(2):
                    y = 2 * (8 * rb + i) + h
                    row = w * lines + y % lines
                    v_ref[y // lines, row : row + 1, :] = v[h][i : i + 1]
                    d_ref[y // lines, row : row + 1, :] = d[h][i : i + 1]


def krylov_kernel(slab, lines, width, group, filtered, parts, before, *refs):
    refs = list(refs)
    take = lambda k: [refs.pop(0) for _ in range(k)]
    flag_ref, d_ref, sh_ref, t_ref = take(4)
    (m_ref,) = take(1) if filtered else (None,)
    packed_refs = take(before)
    o_refs = take(len(parts))
    u_refs = [take(2) for _ in parts]
    (pay_ref,) = take(1)
    v_ref, cs_ref = take(2) if filtered else (t_ref, None)
    (b_s,) = refs
    window = slab + LOW + HIGH
    lane = lax.broadcasted_iota(jnp.int32, (HALF, 128), 1)
    at_low = lane % width == 0
    at_high = lane % width == width - 1
    zero = jnp.zeros((HALF, 128), F32)
    n = t_ref.shape[0]

    if filtered:
        base = window * lines
        total = m_ref[0, base : base + 3, :]
        for k in range(1, n):
            total = total + m_ref[k, base : base + 3, :]
        total = jnp.concatenate([total, jnp.zeros((5, 128), F32)], axis=0)
        total = dot(total, halves(8, width))
        center = total[1:2] / total[0:1]
        inverse = 1.0 / jnp.sqrt(total[2:3] / total[0:1])
        cs_ref[0:1] = center
        cs_ref[1:2] = inverse
        used = v_ref.shape[1]
        for k in range(n):
            v_ref[k] = (m_ref[k, 0:used, :] - center * t_ref[k, 0:used, :]) * inverse

    def v_row(w, y):
        return v_ref[y // lines, pl.ds(w * lines + y % lines, 1), :]

    def d_row(w, y):
        return d_ref[y // lines, pl.ds(w * lines + y % lines, 1), :]

    b_refs = [b_s.at[k] for k in range(len(parts))]
    u1_refs, u2_refs = zip(*u_refs)

    def products(w, carry):
        for y in range(width):
            v = v_row(w, y)
            for b_ref, o_ref in zip(b_refs, o_refs):
                b_ref[w, y] = o_ref[w, y] * v
        return carry

    def apply(srcs, src_at, dsts, dst_at, w, carry, pairs, keep=None):
        fields = [[zero] + [src[w - src_at, y] for y in range(width)] + [zero] for src in srcs]
        terms = [[] for _ in srcs for _ in pairs]
        for y in range(width):
            diag = d_row(w, y)
            for k, (rows, src, dst) in enumerate(zip(fields, srcs, dsts)):
                mid = rows[y + 1]
                around = (rows[y] + rows[y + 2]) + (src[w - 1 - src_at, y] + src[w + 1 - src_at, y])
                around = around + (
                    jnp.where(at_low, 0.0, pltpu.roll(mid, 1, 1))
                    + jnp.where(at_high, 0.0, pltpu.roll(mid, 127, 1))
                )
                new = diag * mid - around
                if keep is not None:
                    new = new * keep
                dst[w - dst_at, y] = new
                both = (mid, new)
                for i, (a, b) in enumerate(pairs):
                    terms[k * len(pairs) + i].append(both[a] * both[b])
        return tuple(old + tree(t) for old, t in zip(carry, terms))

    def last(w, carry):
        fields = [[u2_ref[w - LOW, y] for y in range(width)] + [zero] for u2_ref in u2_refs]
        terms = [[] for _ in fields]
        for y in range(width):
            diag = d_row(w, y)
            for k, (rows, u2_ref) in enumerate(zip(fields, u2_refs)):
                mid = rows[y]
                above = (rows[y + 1] + u2_ref[w + 1 - LOW, y]) + jnp.where(
                    at_high, 0.0, pltpu.roll(mid, 127, 1)
                )
                terms[k].append(mid * (diag * mid - 2.0 * above))
        return tuple(old + tree(t) for old, t in zip(carry, terms))

    first = flag_ref[0]
    own, top = (LOW, LOW + slab), LOW + slab
    inside = {
        LOW - 1: jnp.where(first < 1, 0.0, 1.0),
        top: jnp.where(first + slab >= width, 0.0, 1.0),
        top + 1: jnp.where(first + slab + 1 >= width, 0.0, 1.0),
    }
    lax.fori_loop(0, window, products, 0, unroll=True)
    for w, keep in inside.items():
        apply(b_refs, 0, u1_refs, 1, w, (), (), keep)
    low_pairs, high_pairs = ((0, 0), (0, 1), (1, 1)), ((0, 1), (1, 1))
    lows = lax.fori_loop(
        *own,
        lambda w, c: apply(b_refs, 0, u1_refs, 1, w, c, low_pairs),
        (zero,) * 3 * len(parts),
        unroll=True,
    )
    apply(u1_refs, 1, u2_refs, LOW, top, (), (), inside[top])
    highs = lax.fori_loop(
        *own,
        lambda w, c: apply(u1_refs, 1, u2_refs, LOW, w, c, high_pairs),
        (zero,) * 2 * len(parts),
        unroll=True,
    )
    lasts = lax.fori_loop(*own, last, (zero,) * len(parts), unroll=True)
    column = lax.broadcasted_iota(jnp.int32, (128, 128), 1)
    trial = lax.broadcasted_iota(jnp.int32, (128, 128), 0) // width
    packed = [ref[...] for ref in packed_refs]
    for k, part in enumerate(parts):
        made = sh_ref[part * HALF : (part + 1) * HALF, :]
        moments = (*lows[3 * k : 3 * k + 3], *highs[2 * k : 2 * k + 2], lasts[k])
        for i, moment in enumerate(moments):
            made = made + dot(moment, jnp.where(column == 2 * i + trial, 1.0, 0.0))
        packed.append(made)
    if len(packed) * HALF == ORBS:
        for peer in range(group):
            for k, made in enumerate(packed):
                pay_ref[peer, k * HALF : (k + 1) * HALF, :] = made
    else:
        pay_ref[...] = packed[0]


def combine_kernel(
    slab, lines, width, group, share, flag_ref, pay_ref, v_ref, cy_ref, cz_ref, *refs
):
    o_refs, u_refs = refs[0:2], (refs[2:4], refs[4:6])
    out_ref, field_s = refs[6:]
    chunks = out_ref.shape[0]
    if share:
        rows = share * lines
        for k in range(chunks):
            out_ref[k, slab * lines : slab * lines + rows, :] = v_ref[
                k, pl.ds(flag_ref[2] * rows + LOW * lines, rows), :
            ]
    total = pay_ref[0]
    for k in range(1, group):
        total = total + pay_ref[k]
    row = lax.broadcasted_iota(jnp.int32, (128, 128), 0)
    half = lax.broadcasted_iota(jnp.int32, (128, 128), 1) // width
    m = [dot(total, jnp.where(row == 2 * k + half, 1.0, 0.0)) for k in range(MOMENTS)]
    shift = dot(total, jnp.where(row == SHIFT_LANE, 1.0, 0.0))
    inv = 1.0 / m[0]
    mu = [None] + [m[k] * inv * (8.0**-k) for k in range(1, MOMENTS)]
    sigma = 0.25 * (shift + CENTER)
    k00 = mu[1] + sigma
    k01 = mu[2] + sigma * mu[1]
    k11 = mu[3] + sigma * mu[2]
    k02 = k11
    k12 = mu[4] + sigma * mu[3]
    k22 = mu[5] + sigma * mu[4]
    r0 = 1.0 / k00
    l10 = k01 * r0
    l20 = k02 * r0
    d1 = k11 - l10 * k01
    t = k12 - l20 * k01
    l21 = t / d1
    d2 = k22 - l20 * k02 - l21 * t
    z1 = mu[1] - l10
    z2 = mu[2] - l20 - l21 * z1
    y2 = z2 / d2
    y1 = z1 / d1 - l21 * y2
    y0 = r0 - l10 * y1 - l20 * y2
    c0 = -0.25 * y0
    c1 = (-0.25 / 8.0) * y1
    c2 = (-0.25 / 64.0) * y2

    sublane = lax.broadcasted_iota(jnp.int32, (8, 128), 0)
    takes = [(sublane // step) % 2 == 0 for step in (1, 2, 4)]

    def merge(values):
        for take, step in zip(takes, (1, 2, 4)):
            values = [
                jnp.where(take, a, b) + pltpu.roll(jnp.where(take, b, a), step, 0)
                for a, b in zip(values[::2], values[1::2])
            ]
        return values[0]

    def plane(x, carry):
        w = x + LOW
        for y0 in range(0, width, 8):
            values = []
            for y in range(y0, y0 + 8):
                v = v_ref[y // lines, pl.ds(w * lines + y % lines, 1), :]
                both = []
                for k, (o_ref, (u1_ref, u2_ref)) in enumerate(zip(o_refs, u_refs)):
                    at = slice(k * HALF, (k + 1) * HALF)
                    o = o_ref[w, y]
                    u = c1[at] * u1_ref[x + LOW - 1, y] + c2[at] * u2_ref[x, y]
                    both.append(o * (c0[at] * (o * v) + u))
                values.append(both[0] + both[1])
            field_s[pl.ds(pl.multiple_of(x * width + y0, 8), 8), :] = merge(values)
        return carry

    lax.fori_loop(0, slab, plane, 0)
    turned = dot(field_s[...], cz_ref[...])
    turned = jnp.concatenate([turned[x * width : (x + 1) * width] for x in range(slab)], axis=1)
    planes = dot(cy_ref[...], turned)
    for x in range(slab):
        for k in range(chunks):
            out_ref[k, x * lines : (x + 1) * lines, :] = planes[
                k * lines : (k + 1) * lines, x * 128 : (x + 1) * 128
            ]


def gathered(got_ref, cx_ref, group, crossed):
    n = got_ref.shape[0]
    rows = cx_ref.shape[0] // group
    parts = []
    for j in range(group):
        parts.append(tree([got_ref[q * group + placed(j, crossed), 0:rows, :] for q in range(n // group)]))
    return dot(cx_ref[...], jnp.concatenate(parts, axis=0))


def mapped_kernel(slab, lines, width, group, crossed, got_ref, cx_ref, mapped_ref, t_ref, pay_ref):
    n, size, _ = pay_ref.shape
    mapped = gathered(got_ref, cx_ref, group, crossed)
    mapped_ref[...] = mapped
    rounds = n // group
    rows = slab // rounds * lines
    for j in range(group):
        for q in range(rounds):
            at = (j * rounds + q) * rows
            t_ref[at : at + rows, :] = got_ref[q * group + placed(j, crossed), slab * lines : slab * lines + rows, :]
    t = t_ref[...]
    sums = [jnp.sum(a * b, axis=0, keepdims=True) for a, b in ((t, t), (t, mapped), (mapped, mapped))]
    window = (slab + LOW + HIGH) * lines
    for k in range(n):
        start = placed(k % group, crossed) * slab * lines - LOW * lines
        low, high = max(start, 0), min(start + window, width * lines)
        pay_ref[k] = jnp.zeros((size, 128), F32)
        pay_ref[k, low - start : high - start, :] = mapped_ref[low:high, :]
        for i, s in enumerate(sums):
            pay_ref[k, window + i : window + i + 1, :] = s


def second_kernel(group, crossed, got_ref, cx_ref, t_ref, mapped_ref, cs_ref, second_ref):
    again = gathered(got_ref, cx_ref, group, crossed)
    center, inverse = cs_ref[0:1], cs_ref[1:2]
    t = t_ref[...]
    first = (mapped_ref[...] - center * t) * inverse
    second_ref[...] = 2.0 * (again - center * first) * inverse - t


def turn(x):
    return pltpu.roll(x, 64, x.ndim - 1)


def gram_kernel(per, second_ref, other_ref, pay_ref):
    n, size, _ = pay_ref.shape
    a, b = second_ref[...], other_ref[...]
    a1, b1 = turn(a), turn(b)
    pairs = ((a, a), (a, a1), (a, b), (a, b1), (b, b), (b, b1))
    sums = [jnp.sum(p * q, axis=0, keepdims=True) for p, q in pairs]
    block = jnp.concatenate(sums + [jnp.zeros((8 - len(sums), 128), F32)], axis=0)
    for k in range(n):
        pay_ref[k, 0:per, :] = second_ref[k * per : (k + 1) * per, :]
        pay_ref[k, size - 8 : size, :] = block


def final_kernel(per, width, flag_ref, got_ref, other_ref, out_ref, rows_s):
    n, size, _ = got_ref.shape
    total = tree([got_ref[k, size - 8 : size, :] for k in range(n)])
    total = dot(total, halves(8, width)) / float(width**3)
    swapped = turn(total)
    lane = lax.broadcasted_iota(jnp.int32, (1, 128), 1)
    in_first = lane < width
    is_low = jnp.zeros((1, 128), jnp.int32) + flag_ref[1] == 0

    def entry(k, t):
        here, there = total[k : k + 1], swapped[k : k + 1]
        return jnp.where(in_first, here, there) if t == 0 else jnp.where(in_first, there, here)

    aa = ((entry(0, 0), entry(1, 0)), (entry(1, 0), entry(0, 1)))
    bb = ((entry(4, 0), entry(5, 0)), (entry(5, 0), entry(4, 1)))
    ab = ((entry(2, 0), entry(3, 0)), (entry(3, 1), entry(2, 1)))
    m = [[None] * 4 for _ in range(4)]
    for i in range(2):
        for j in range(2):
            m[i][j] = jnp.where(is_low, aa[i][j], bb[i][j])
            m[2 + i][2 + j] = jnp.where(is_low, bb[i][j], aa[i][j])
            m[2 + j][i] = jnp.where(is_low, ab[i][j], ab[j][i])
    low = [[None] * 4 for _ in range(4)]
    inv = [[jnp.zeros((1, 128), F32)] * 4 for _ in range(4)]
    for j in range(4):
        pivot = m[j][j]
        for k in range(j):
            pivot = pivot - low[j][k] * low[j][k]
        inv[j][j] = 1.0 / jnp.sqrt(pivot)
        for i in range(j + 1, 4):
            value = m[i][j]
            for k in range(j):
                value = value - low[i][k] * low[j][k]
            low[i][j] = value * inv[j][j]
    for j in range(4):
        for i in range(j + 1, 4):
            value = low[i][j] * inv[j][j]
            for k in range(j + 1, i):
                value = value + low[i][k] * inv[k][j]
            inv[i][j] = -value * inv[i][i]

    def pick(i, j):
        return jnp.where(is_low, inv[i][j], inv[2 + i][(j + 2) % 4])

    c = [
        jnp.where(in_first, pick(0, a), pick(1, b)) for a, b in ((0, 1), (1, 0), (2, 3), (3, 2))
    ]
    for k in range(n):
        a, b = got_ref[k, 0:per, :], other_ref[k]
        rows_s[k] = (c[0] * a + c[1] * turn(a)) + (c[2] * b + c[3] * turn(b))
    planes = out_ref.shape[1]
    first_half = lax.broadcasted_iota(jnp.int32, (planes, 128), 1) < width
    lines = per // planes

    def line(y):
        return rows_s[y // lines, pl.ds(y % lines, planes, stride=lines), :]

    for pair in range(width // 2):
        even, odd = line(2 * pair), line(2 * pair + 1)
        at = slice(pair * 128, (pair + 1) * 128)
        out_ref[0, :, at] = jnp.where(first_half, even, turn(odd))
        out_ref[1, :, at] = jnp.where(first_half, turn(even), odd)


def vmem():
    return pl.BlockSpec(memory_space=pltpu.VMEM)


def smem():
    return pl.BlockSpec(memory_space=pltpu.SMEM)


def call(kernel, name, shapes, inputs, scratch=(), limit=4, in_smem=()):
    return pl.pallas_call(
        kernel,
        out_shape=shapes,
        in_specs=[smem() if k in in_smem else vmem() for k in range(len(inputs))],
        out_specs=jax.tree.map(lambda _: vmem(), shapes),
        scratch_shapes=scratch,
        compiler_params=pltpu.CompilerParams(vmem_limit_bytes=limit * MIB),
        name=name,
    )(*inputs)


def shape(*dims):
    return jax.ShapeDtypeStruct(dims, F32)


def up8(x):
    return -(-x // 8) * 8


def shards(n, cores, trials, orbitals, potential, coulomb, energies, frequencies, orbital_ids, freq_index):
    count, planes, cells = trials.shape
    held = orbitals.shape[0]
    width = coulomb.shape[1]
    lines = width // n
    group = ORBS // held
    slab = width // group
    window = slab + LOW + HIGH
    me = lax.axis_index("orb")
    core = lax.axis_index("trial")
    place = me % group
    direct = planes >= HIGH and n // group == 2
    crossed = direct and group == 8
    pairs = cells // 128
    each = held // cores
    groups = [list(range(q * group, (q + 1) * group)) for q in range(n // group)]

    def swap(x):
        return lax.ppermute(x, "trial", [(k, (k + 1) % cores) for k in range(cores)])

    def exchange(x):
        return lax.all_to_all(x, "orb", split_axis=0, concat_axis=0, tiled=True)

    def exchange_group(x):
        return lax.all_to_all(
            x, "orb", split_axis=0, concat_axis=0, tiled=True, axis_index_groups=groups
        )

    mine = lax.dynamic_slice_in_dim(orbitals, core * each, each, 0).astype(F32)
    mine = mine.reshape(each, width * pairs, 128)
    sent = call(
        functools.partial(pack_kernel, slab, window, width, pairs, crossed),
        "pack_orbitals",
        shape(group, each * window * pairs, 128),
        (mine,),
        limit=8,
    )
    own_half = exchange_group(sent)
    own_half = own_half.reshape(HALF * window * pairs, 128)
    shifts = orbital_shifts(orbital_ids, freq_index, energies, frequencies)
    shifts = jnp.where(core == 0, shifts, jnp.roll(shifts, -each))
    slot_rows = [(k // each) * HALF + place * each + k % each for k in range(held)]
    row = lax.broadcasted_iota(jnp.int32, (ORBS, 128), 0)
    lane = lax.broadcasted_iota(jnp.int32, (ORBS, 128), 1)
    shift_rows = sum(
        jnp.where((row == slot_rows[k]) & (lane == SHIFT_LANE), shifts[k], 0.0) for k in range(held)
    )

    rounds = n // group
    flags = jnp.stack([placed(place, crossed) * slab, core, me // group]).astype(jnp.int32)
    fields = jnp.concatenate([trials, potential[None]], axis=0).reshape(count + 1, planes * pairs, 128)
    blocks = [
        lax.ppermute(
            fields,
            "orb",
            [
                (j * rounds + k, (k + r) % rounds * group + placed(j, crossed))
                for j in range(group)
                for k in range(rounds)
            ],
        )
        for r in range(rounds)
    ]
    slabs = call(
        functools.partial(slab_kernel, rounds),
        "slab",
        shape(count + 1, slab * pairs, 128),
        (flags, *blocks),
        limit=8,
        in_smem=(0,),
    )
    if direct:
        last = me % rounds == rounds - 1
        edge = jnp.where(last, fields[:, (planes - HIGH) * pairs :], fields[:, : HIGH * pairs])
        first, other = (
            lax.ppermute(
                edge,
                "orb",
                [((j - 1) * rounds + 1, q * group + placed(j, crossed)) for j in range(1, group)]
                + [((j + 1) * rounds, (1 - q) * group + placed(j, crossed)) for j in range(group - 1)],
            )
            for q in range(rounds)
        )
        is_first = me // group == 0
        low = jnp.where(is_first, first, other)[:, (HIGH - LOW) * pairs :]
        high = jnp.where(is_first, other, first)
    else:
        low = lax.ppermute(
            slabs[:, (slab - LOW) * pairs :], "orb", [(i, i + 1) for i in range(n) if i % group < group - 1]
        )
        high = lax.ppermute(slabs[:, : HIGH * pairs], "orb", [(i, i - 1) for i in range(n) if i % group > 0])
    used = window * lines
    trial_window, diag_window = call(
        functools.partial(fields_kernel, slab, lines, pairs),
        "fields",
        (shape(n, used, 128), shape(n, used, 128)),
        (slabs, low, high),
        limit=8,
    )
    cy = coulomb[1]
    cx, cz = call(
        functools.partial(factors_kernel, lines, width),
        "factors",
        (shape(width * lines, width * lines), shape(128, 128)),
        (coulomb,),
    )
    trial_window, diag_window, cx, cy, cz, shift_rows, own_half = lax.optimization_barrier(
        (trial_window, diag_window, cx, cy, cz, shift_rows, own_half)
    )
    spread_orbitals = [
        call(
            functools.partial(spread_kernel, window, pairs),
            "spread_orbitals",
            shape(window, width, HALF, 128),
            (rows,),
            scratch=[pltpu.VMEM((HALF * (window * pairs + 1), 128), F32)],
        )
        for rows in (own_half, swap(own_half))
    ]

    def krylov(parts, fields, packed):
        filtered = len(fields) == 2
        complete = len(packed) + len(parts) == 2
        shapes = [shape(slab + 3, width, HALF, 128), shape(slab + 1, width, HALF, 128)] * len(parts)
        shapes.append(shape(group, ORBS, 128) if complete else shape(HALF, 128))
        if filtered:
            shapes += [shape(n, used, 128), shape(8, 128)]
        return call(
            functools.partial(krylov_kernel, slab, lines, width, group, filtered, parts, len(packed)),
            "krylov",
            tuple(shapes),
            (flags, diag_window, shift_rows, *fields, *packed, *[spread_orbitals[k] for k in parts]),
            scratch=[pltpu.VMEM((len(parts), window, width, HALF, 128), F32)],
            limit=14,
            in_smem=(0,),
        )

    def combine(pay, v, us, share):
        part = call(
            functools.partial(combine_kernel, slab, lines, width, group, share),
            "combine",
            shape(n, up8((slab + share) * lines), 128),
            (flags, exchange_group(pay), v, cy, cz, *spread_orbitals, *us),
            scratch=[pltpu.VMEM((slab * width, 128), F32)],
            limit=4,
            in_smem=(0,),
        )
        return exchange(part)

    own_u1, own_u2, packed = krylov((0,), (trial_window,), ())
    other_u1, other_u2, pay = krylov((1,), (trial_window,), (packed,))
    got = combine(pay, trial_window, (own_u1, own_u2, other_u1, other_u2), slab // rounds)
    mapped, trial_rows, pay = call(
        functools.partial(mapped_kernel, slab, lines, width, group, crossed),
        "mapped",
        (shape(width * lines, 128), shape(width * lines, 128), shape(n, up8(used + 3), 128)),
        (got, cx),
    )
    made = krylov((0, 1), (trial_window, exchange(pay)), ())
    pay, v, scales = made[4:]
    got = combine(pay, v, made[:4], 0)
    second = call(
        functools.partial(second_kernel, group, crossed),
        "second",
        shape(width * lines, 128),
        (got, cx, trial_rows, mapped, scales),
    )
    per = planes * lines
    pay = call(functools.partial(gram_kernel, per), "gram", shape(n, up8(per) + 8, 128), (second, swap(second)))
    got = exchange(pay)
    return call(
        functools.partial(final_kernel, per, width),
        "final",
        shape(count, planes, cells),
        (flags, got, swap(got[:, :per])),
        scratch=[pltpu.VMEM((n, per, 128), F32)],
        in_smem=(0,),
    )


def solution(mesh):
    n, cores = mesh.shape["orb"], mesh.shape["trial"]
    in_specs = (
        P("trial", "orb", None), P("orb", None, None), P("orb", None), P(), P(), P(), P("orb"), P("orb"),
    )
    return jax.shard_map(
        functools.partial(shards, n, cores),
        mesh=mesh, in_specs=in_specs, out_specs=P("trial", "orb", None), check_vma=False,
    )
```
